256 devices in a mesh: grp: 4 (over x), dev: 64 (over z, y, core).
Axes of the slice: x: 4, y: 4, z: 8, core: 2. Of those that a mesh axis runs over, the one named last changes fastest.
Arguments:
- design: float32 [524288, 256], P(('grp', 'dev')), may hold values from -6 to 6
- sign_bits: int32 [524288], P(('grp', 'dev')), may hold values from 0 to 1
- sample_rows: int32 [4, 8192], P('grp'), may hold values from 0 to 131071, as said below
Outputs:
- sketch_rows: float32 [32768, 256], P(('grp', 'dev'))
- gram: float32 [256, 256], replicated
The draws below stay inside these ranges and needn't reach their ends.
Inputs may be any that keep to these rules, and one draw needn't show every extreme that they name: `sample_rows`: split each slab's samples into 64 blocks of 128 in order, and the rows r of a slab into 64 ranges by (r % 2048) // 32. In every block each range holds either exactly 4 samples or none; rows may repeat.
All inputs are finite; a program needn't handle non-finite values.
Results may differ from the reference program's by a relative error of at most 0.0001.
Values sent between devices are 32-bit elements; how exact they have to be, the bound alone decides.
A program may use at most 64 MiB of HBM per device.

```python
import math
import jax
import jax.numpy as jnp
from jax import lax

D = 256
ROWS_DEV = 2048
SAMP_DEV = 128
SLAB = 131072
SAMPLES = 8192
N_GRP = 4
N_DEV = 64


def draw_sample_rows(key, part):
    key = jax.random.fold_in(key, 11)
    keys = jax.random.split(key, 5)
    owners_per = min(N_DEV, 32)
    per_owner = SAMP_DEV // owners_per
    range_rows = ROWS_DEV // N_DEV
    favored = (jax.random.randint(keys[0], (N_GRP, 1, N_DEV), 0, 4) == 0).astype(jnp.int32)
    scores = jax.random.randint(keys[1], (N_GRP, N_DEV, N_DEV), 0, 4 * N_DEV) - 3 * N_DEV * favored
    scores = scores * N_DEV + jnp.arange(N_DEV, dtype=jnp.int32)
    chosen = jnp.argsort(scores, axis=-1)[..., :owners_per].astype(jnp.int32)
    repeated = jnp.repeat(chosen, per_owner, axis=-1)
    shuffle_keys = jax.random.randint(keys[2], (N_GRP, N_DEV, SAMP_DEV), 0, SAMP_DEV) * SAMP_DEV + jnp.arange(SAMP_DEV, dtype=jnp.int32)
    order = jnp.argsort(shuffle_keys, axis=-1)
    owners = jnp.take_along_axis(repeated, order, axis=-1)
    source = jax.random.randint(keys[3], (N_GRP, N_DEV, SAMP_DEV), 0, N_DEV)
    offset = jax.random.randint(keys[4], (N_GRP, N_DEV, SAMP_DEV), 0, range_rows)
    rows = source * ROWS_DEV + owners * range_rows + offset
    return rows.reshape(N_GRP, N_DEV * SAMP_DEV).astype(jnp.int32)


def place_ends(result, rng, low, largest):
    extent = result.shape
    place = [jax.random.randint(jax.random.fold_in(rng, axis), (), 0, extent[axis]) for axis in range(len(extent))]
    result = result.at[tuple(place)].set(low)
    longest = extent.index(max(extent))
    place[longest] = (place[longest] + 1) % extent[longest]
    return result.at[tuple(place)].set(largest)


def shard_levels(rng, extent, cuts, smallest, high):
    gain, own = 1.0, jax.random.fold_in(rng, 6)
    for position, parts in cuts:
        steps = jnp.exp(jax.random.uniform(jax.random.fold_in(own, position), (parts,), jnp.float32, smallest / len(cuts), high / len(cuts)))
        gain = gain * jnp.repeat(steps, extent[position] // parts).reshape([-1 if axis == position else 1 for axis in range(len(extent))])
    return gain


def gaussian(own_key, extent, spread, most, cuts=(), kind=jnp.bfloat16):
    array = spread * jax.random.normal(own_key, extent, jnp.float32)
    if cuts:
        array = array * shard_levels(own_key, extent, cuts, -0.22, 0.18)
    return jnp.clip(array, -most, most).astype(kind)


def setup_inputs(seed: int = 0) -> dict:
    splits = jax.random.split(jax.random.key(seed), 4)
    return {
        "design": gaussian(splits[0], (N_GRP * SLAB, D), 1.0, 6.0, ((0, 256),), jnp.float32),
        "sign_bits": place_ends(jax.random.randint(splits[1], (N_GRP * SLAB,), 0, 2), jax.random.fold_in(splits[1], 1), 0, 1).astype(jnp.int32),
        "sample_rows": draw_sample_rows(jax.random.fold_in(splits[3], 71), 0),
    }


def walsh_table(length):
    row_ids = jnp.arange(length, dtype=jnp.int32)[:, None]
    col_ids = jnp.arange(length, dtype=jnp.int32)[None, :]
    parity = jnp.zeros((length, length), jnp.int32)
    for level in range(length.bit_length() - 1):
        both = jnp.bitwise_and(jnp.right_shift(row_ids, level), 1) * jnp.bitwise_and(jnp.right_shift(col_ids, level), 1)
        parity = jnp.bitwise_xor(parity, both)
    return (1 - 2 * parity).astype(jnp.float32)

def walsh_apply(values, length):
    if length <= 128:
        return jnp.dot(walsh_table(length), values, precision=lax.Precision.HIGHEST, preferred_element_type=jnp.float32)
    factor = 128
    rest = length // factor
    columns = values.shape[1]
    blocks = values.reshape(rest, factor, columns)
    blocks = jnp.einsum('ij,ajc->aic', walsh_table(factor), blocks, precision=lax.Precision.HIGHEST)
    return walsh_apply(blocks.reshape(rest, factor * columns), rest).reshape(length, columns)

def reference(design, sign_bits, sample_rows):
    slab = ROWS_DEV * N_DEV
    scale = 1.0 / math.sqrt(slab)
    pieces = []
    for group in range(N_GRP):
        signs = (2 * sign_bits[group * slab:(group + 1) * slab] - 1).astype(jnp.float32)
        signed = design[group * slab:(group + 1) * slab] * signs[:, None]
        mixed = walsh_apply(signed, slab) * scale
        pieces.append(jnp.take(mixed, sample_rows[group], axis=0))
    sketch_rows = jnp.concatenate(pieces, axis=0)
    gram = jnp.dot(sketch_rows.T, sketch_rows, precision=lax.Precision.HIGHEST, preferred_element_type=jnp.float32)
    gram = gram / float(N_GRP * SAMPLES)
    return (sketch_rows, gram)
```

```python
import functools
import math

import jax
import jax.numpy as jnp
from jax import lax
from jax.experimental import pallas as pl
from jax.experimental.pallas import tpu as pltpu
from jax.sharding import PartitionSpec as P

MESH = pl.DeviceIdType.MESH
F32 = jnp.float32
BF16 = jnp.bfloat16

PLANES = 8
PEERS = 8
CHUNKS = 8
IN_RANGE = 32
SLOTS = 4
BLOCKS = 64
HOLDERS = 32
LAG = 2


def butterfly(parts):
    span = 1
    while span < len(parts):
        out = list(parts)
        for a in range(len(parts)):
            if a & span == 0:
                out[a] = parts[a] + parts[a + span]
                out[a + span] = parts[a] - parts[a + span]
        parts = out
        span *= 2
    return parts


def split2(value):
    high = value.astype(BF16)
    return high, (value - high.astype(F32)).astype(BF16)


def dot(a, b):
    return jnp.dot(a, b, preferred_element_type=F32)


def dot_first(a, b):
    return lax.dot_general(a, b, (((0,), (0,)), ((), ())), preferred_element_type=F32)


def kernel(
    scale, gram_scale,
    design, bits, samples, sketch, gram,
    held, signs, table, arrived, partial, ring, code, owner, code_wide, pick,
    staged, slots, local, part_in, z_in,
    load_sem, y_send, y_recv, z_send, z_recv, d_send, d_recv,
    a_send, a_recv, b_send, b_recv, c_send, c_recv,
):
    g = lax.axis_index("grp")
    dev = lax.axis_index("dev")
    z = dev // PEERS
    p = dev % PEERS
    holder = g * PEERS + p

    def holder_id(k):
        other = holder ^ k
        return (other // PEERS, z * PEERS + other % PEERS)

    load = pltpu.make_async_copy(design, held, load_sem)
    load.start()

    barrier = pltpu.get_barrier_semaphore()
    for k in range(1, PLANES):
        pl.semaphore_signal(barrier, inc=1, device_id=(g, (z ^ k) * PEERS + p), device_id_type=MESH)

    def greet(k, carry):
        pl.semaphore_signal(barrier, inc=1, device_id=holder_id(k), device_id_type=MESH)
        return carry

    lax.fori_loop(1, HOLDERS, greet, 0)

    lane = lax.broadcasted_iota(jnp.int32, (128, 128), 1)
    row = lax.broadcasted_iota(jnp.int32, (128, 128), 0)
    ones = jnp.ones((128, 128), BF16)
    for i in range(16):
        sign = (2 * bits[pl.ds(i, 1), :] - 1).astype(F32)
        diagonal = jnp.where(lane == row, jnp.broadcast_to(sign, (128, 128)), 0.0)
        signs[pl.ds(i * 128, 128), :] = dot(diagonal.astype(BF16), ones)

    target = samples[...]
    owner[...] = (target >> 5) & 63
    along_z = (target >> 14) & z
    flip = (along_z ^ (along_z >> 1) ^ (along_z >> 2)) & 1
    code[...] = ((((target >> 11) & 7) << 5) | (target & 31) | (flip << 8) | 512).astype(F32)

    load.wait()

    def high_bits(i, carry):
        base = pl.multiple_of(i * IN_RANGE, IN_RANGE)
        for half in range(2):
            cols = pl.ds(half * 128, 128)
            parts = [
                held[pl.ds(k * 256 + base, IN_RANGE), cols] * signs[pl.ds(k * 256 + base, IN_RANGE), :]
                for k in range(8)
            ]
            for k, value in enumerate(butterfly(parts)):
                held[pl.ds(k * 256 + base, IN_RANGE), cols] = value
        return carry

    lax.fori_loop(0, 8, high_bits, 0)
    pl.semaphore_wait(barrier, PLANES - 1 + HOLDERS - 1)

    def y_copy(j, k):
        peer = p ^ k
        return pltpu.make_async_remote_copy(
            held.at[pl.ds(pl.multiple_of(j * 256 + peer * IN_RANGE, IN_RANGE), IN_RANGE)],
            arrived.at[j, pl.ds(pl.multiple_of(p * IN_RANGE, IN_RANGE), IN_RANGE)],
            y_send.at[j, k], y_recv.at[j, k],
            device_id=(g, z * PEERS + peer), device_id_type=MESH,
        )

    def y_landed(j, k):
        peer = p ^ k
        return pltpu.make_async_remote_copy(
            held.at[pl.ds(pl.multiple_of(j * 256 + p * IN_RANGE, IN_RANGE), IN_RANGE)],
            arrived.at[j, pl.ds(pl.multiple_of(peer * IN_RANGE, IN_RANGE), IN_RANGE)],
            y_send.at[j, k], y_recv.at[j, k],
            device_id=(g, z * PEERS + peer), device_id_type=MESH,
        )

    def low_bits(j, carry):
        base = pl.multiple_of(j * 256, 256)
        for half in range(2):
            cols = pl.ds(half * 128, 128)
            parts = [held[pl.ds(base + k * IN_RANGE, IN_RANGE), cols] for k in range(8)]
            for k, value in enumerate(butterfly(parts)):
                held[pl.ds(base + k * IN_RANGE, IN_RANGE), cols] = value
        for k in (4, 5, 2, 3, 6, 7, 1):
            y_copy(j, k).start()
        mine = pl.multiple_of(p * IN_RANGE, IN_RANGE)
        arrived[j, pl.ds(mine, IN_RANGE), :] = held[pl.ds(base + mine, IN_RANGE), :]
        return carry

    lax.fori_loop(0, CHUNKS, low_bits, 0)

    before = (row < lane).astype(BF16)

    def build(j, carry):
        here = owner[...] == 8 * j + p
        rank = dot(here.astype(F32).astype(BF16), before)
        for i in range(SLOTS):
            chosen = jnp.where(here & (rank == float(i)), code[...], 0.0)
            column = jnp.sum(chosen, axis=1, keepdims=True)
            code_wide[pl.ds(i, BLOCKS, stride=SLOTS), :] = jnp.broadcast_to(column, (BLOCKS, 128))
        wide = code_wide[...].astype(jnp.int32)
        at = lax.broadcasted_iota(jnp.int32, (256, 128), 1) + 256
        for half in range(2):
            v = wide & (at + 128 * half)
            v = v ^ (v >> 8)
            v = v ^ (v >> 4)
            v = v ^ (v >> 2)
            v = v ^ (v >> 1)
            value = jnp.where(wide >= 512, 1 - 2 * (v & 1), 0).astype(F32)
            table[j, :, pl.ds(half * 128, 128)] = value.astype(BF16)
        return carry

    lax.fori_loop(0, CHUNKS, build, 0)

    own = jnp.broadcast_to((samples[pl.ds(dev, 1), :] >> 5) & 63, (128, 128)).astype(F32)
    same = jnp.where((own == own.T) & (row < lane), 1.0, 0.0)
    rank = jnp.broadcast_to(jnp.sum(same, axis=0, keepdims=True), (128, 128))
    own = own.astype(jnp.int32)
    place = ((own & 7) * 32 + (own >> 3) * 4).astype(F32) + rank
    place = place.T
    for half in range(2):
        at = (lane + 128 * half).astype(F32)
        pick[:, pl.ds(half * 128, 128)] = jnp.where(place == at, 1.0, 0.0).astype(BF16)

    local[...] = jnp.zeros_like(local)

    def block(index):
        return pl.ds(pl.multiple_of(index * 32, 32), 32)

    def hop(j, way, step, source):
        step_z = 1 if way == 0 else PLANES - 1
        return pltpu.make_async_remote_copy(
            source, ring.at[j, way, step], z_send.at[j, way, step], z_recv.at[j, way, step],
            device_id=(g, (z + step_z) % PLANES * PEERS + p), device_id_type=MESH,
        )

    def reach(j, way):
        return 3 + (j + way + 1) % 2

    def dest(j, way, step):
        far = reach(j, way) - step
        return (z + far) % PLANES if way == 0 else (z + PLANES - far) % PLANES

    def produce(j):
        for k in range(1, PEERS):
            y_landed(j, k).wait_recv()
        high, low = split2(arrived[j])
        partial[j] = dot(table[j], high) + dot(table[j], low)
        for way in range(2):
            hop(j, way, 0, partial.at[j, block(dest(j, way, 0))]).start()

    def deliver(m, k):
        peer = p ^ k
        return pltpu.make_async_remote_copy(
            staged.at[m, peer], slots.at[pl.ds(pl.multiple_of(p * 32 + m * 8, 8), 8)],
            d_send.at[m, k], d_recv.at[m, k],
            device_id=(g, z * PEERS + peer), device_id_type=MESH,
        )

    def delivered(m, k):
        peer = p ^ k
        return pltpu.make_async_remote_copy(
            staged.at[m, p], slots.at[pl.ds(pl.multiple_of(peer * 32 + m * 8, 8), 8)],
            d_send.at[m, k], d_recv.at[m, k],
            device_id=(g, z * PEERS + peer), device_id_type=MESH,
        )

    def forward(j, step):
        for way in range(2):
            def take(way=way):
                hop(j, way, step - 1, partial.at[j, block(0)]).wait_recv()

            def send(way=way):
                ring[j, way, step - 1] += partial[j, block(dest(j, way, step)), :]
                hop(j, way, step, ring.at[j, way, step - 1]).start()

            if step <= 2:
                take()
                send()
            elif step == 3:
                take()
                pl.when(reach(j, way) == 4)(send)
            else:
                pl.when(reach(j, way) == 4)(take)

    def finish(j):
        done = partial[j, block(z), :]
        for way in range(2):
            done = done + ring[j, way, reach(j, way) - 1]
        m = j // 2
        for odd in range(2):

            @pl.when(j % 2 == odd)
            def _(odd=odd):
                for k in range(PEERS):
                    staged[m, k, pl.ds(odd * SLOTS, SLOTS), :] = done[k * SLOTS : (k + 1) * SLOTS, :]

        high, low = split2(done)
        local[...] += dot_first(high, high) + dot_first(high, low) + dot_first(low, high)

        @pl.when(j % 2 == 1)
        def _():
            for k in (4, 5, 2, 3, 6, 7, 1):
                deliver(m, k).start()
            slots[pl.ds(pl.multiple_of(p * 32 + m * 8, 8), 8), :] = staged[m, p]

    def turn(t, carry):
        @pl.when(t < CHUNKS)
        def _():
            produce(t)

        for step in range(1, 5):
            j = t - LAG * step

            @pl.when((j >= 0) & (j < CHUNKS))
            def _(j=j, step=step):
                forward(j, step)
                if step == 4:
                    finish(j)

        return carry

    lax.fori_loop(0, CHUNKS + 4 * LAG, turn, 0)

    def rows(index):
        return pl.ds(pl.multiple_of(index * 8, 8), 8)

    def copy_a(k):
        return pltpu.make_async_remote_copy(
            local.at[rows(holder ^ k)], part_in.at[holder], a_send.at[k], a_recv.at[k],
            device_id=holder_id(k), device_id_type=MESH,
        )

    def landed_a(k):
        return pltpu.make_async_remote_copy(
            local.at[rows(holder)], part_in.at[holder ^ k], a_send.at[k], a_recv.at[k],
            device_id=holder_id(k), device_id_type=MESH,
        )

    def copy_b(k):
        return pltpu.make_async_remote_copy(
            z_in.at[z], z_in.at[z], b_send.at[k], b_recv.at[k],
            device_id=(g, (z ^ k) * PEERS + p), device_id_type=MESH,
        )

    def landed_b(k):
        return pltpu.make_async_remote_copy(
            z_in.at[z], z_in.at[z ^ k], b_send.at[k], b_recv.at[k],
            device_id=(g, (z ^ k) * PEERS + p), device_id_type=MESH,
        )

    def copy_c(k):
        return pltpu.make_async_remote_copy(
            gram.at[rows(holder)], gram.at[rows(holder)], c_send.at[k], c_recv.at[k],
            device_id=holder_id(k), device_id_type=MESH,
        )

    def landed_c(k):
        return pltpu.make_async_remote_copy(
            gram.at[rows(holder)], gram.at[rows(holder ^ k)], c_send.at[k], c_recv.at[k],
            device_id=holder_id(k), device_id_type=MESH,
        )

    def each(start, stop, act):
        def step(k, carry):
            act(k)
            return carry

        lax.fori_loop(start, stop, step, 0)

    each(1, HOLDERS, lambda k: copy_a(HOLDERS - k).start())

    part_in[holder] = local[rows(holder), :]
    for m in range(CHUNKS // 2):
        for k in range(1, PEERS):
            delivered(m, k).wait_recv()
    value = slots[...]
    first, rest = split2(value)
    second, third = split2(value - first.astype(F32))
    sketch[...] = (dot(pick[...], first) + dot(pick[...], second) + dot(pick[...], third)) * scale

    each(1, HOLDERS, lambda k: landed_a(k).wait_recv())
    z_in[z] = jnp.sum(part_in[...], axis=0)
    each(1, PLANES, lambda k: copy_b(PLANES - k).start())
    each(1, PLANES, lambda k: landed_b(k).wait_recv())
    gram[rows(holder), :] = jnp.sum(z_in[...], axis=0) * gram_scale
    each(1, HOLDERS, lambda k: copy_c(HOLDERS - k).start())
    each(1, HOLDERS, lambda k: landed_c(k).wait_recv())

    def y_sent(j, carry):
        for k in range(1, PEERS):
            y_copy(j, k).wait_send()
        for way in range(2):
            for step in range(3):
                hop(j, way, step, ring.at[j, way, step]).wait_send()

            @pl.when(reach(j, way) == 4)
            def _(way=way):
                hop(j, way, 3, ring.at[j, way, 2]).wait_send()
        return carry

    lax.fori_loop(0, CHUNKS, y_sent, 0)
    for m in range(CHUNKS // 2):
        for k in range(1, PEERS):
            deliver(m, k).wait_send()
    each(1, HOLDERS, lambda k: copy_a(k).wait_send())
    each(1, PLANES, lambda k: copy_b(k).wait_send())
    each(1, HOLDERS, lambda k: copy_c(k).wait_send())


def shards(design, sign_bits, sample_rows):
    rows, width = design.shape
    slab = rows * lax.axis_size("dev")
    total = lax.axis_size("grp") * sample_rows.shape[1]
    vmem = pl.BlockSpec(memory_space=pltpu.VMEM)
    dma = pltpu.SemaphoreType.DMA
    return pl.pallas_call(
        functools.partial(kernel, 1.0 / math.sqrt(slab), 1.0 / (slab * total)),
        out_shape=(
            jax.ShapeDtypeStruct((128, width), F32),
            jax.ShapeDtypeStruct((width, width), F32),
        ),
        in_specs=[pl.BlockSpec(memory_space=pl.ANY), vmem, vmem],
        out_specs=(vmem, vmem),
        scratch_shapes=[
            pltpu.VMEM((2048, 256), F32),
            pltpu.VMEM((2048, 128), F32),
            pltpu.VMEM((CHUNKS, 256, 256), BF16),
            pltpu.VMEM((CHUNKS, 256, 256), F32),
            pltpu.VMEM((CHUNKS, 256, 256), F32),
            pltpu.VMEM((CHUNKS, 2, 4, 32, 256), F32),
            pltpu.VMEM((BLOCKS, 128), F32),
            pltpu.VMEM((BLOCKS, 128), jnp.int32),
            pltpu.VMEM((256, 128), F32),
            pltpu.VMEM((128, 256), BF16),
            pltpu.VMEM((CHUNKS // 2, PEERS, 8, 256), F32),
            pltpu.VMEM((256, 256), F32),
            pltpu.VMEM((256, 256), F32),
            pltpu.VMEM((HOLDERS, 8, 256), F32),
            pltpu.VMEM((PLANES, 8, 256), F32),
            dma,
            dma((CHUNKS, PEERS)), dma((CHUNKS, PEERS)),
            dma((CHUNKS, 2, 4)), dma((CHUNKS, 2, 4)),
            dma((CHUNKS // 2, PEERS)), dma((CHUNKS // 2, PEERS)),
            dma((HOLDERS,)), dma((HOLDERS,)),
            dma((PLANES,)), dma((PLANES,)),
            dma((HOLDERS,)), dma((HOLDERS,)),
        ],
        compiler_params=pltpu.CompilerParams(
            collective_id=0, has_side_effects=True, vmem_limit_bytes=32 << 20
        ),
        cost_estimate=pl.CostEstimate(flops=2 * 10**9, bytes_accessed=4 << 20, transcendentals=0),
    )(design, sign_bits.reshape(16, 128), sample_rows.reshape(BLOCKS, 128))


def solution(mesh):
    return jax.shard_map(
        shards,
        mesh=mesh,
        in_specs=(P(("grp", "dev"), None), P(("grp", "dev")), P("grp", None)),
        out_specs=(P(("grp", "dev"), None), P()),
        check_vma=False,
    )
```

```python
import functools
import math

import jax
import jax.numpy as jnp
from jax import lax
from jax.experimental import pallas as pl
from jax.experimental.pallas import tpu as pltpu
from jax.sharding import PartitionSpec as P

MESH = pl.DeviceIdType.MESH
F32 = jnp.float32
BF16 = jnp.bfloat16

GROUPS = 4
PLANES = 8
PEERS = 8
CHUNKS = 8
IN_RANGE = 32
SLOTS = 4
BLOCKS = 64
HOLDERS = 32
FAR_FIRST = tuple(k ^ 20 for k in range(HOLDERS) if k != 20)
LAG = 2


def butterfly(parts):
    span = 1
    while span < len(parts):
        out = list(parts)
        for a in range(len(parts)):
            if a & span == 0:
                out[a] = parts[a] + parts[a + span]
                out[a + span] = parts[a] - parts[a + span]
        parts = out
        span *= 2
    return parts


def split2(value):
    high = value.astype(BF16)
    return high, (value - high.astype(F32)).astype(BF16)


def dot(a, b):
    return jnp.dot(a, b, preferred_element_type=F32)


def dot_first(a, b):
    return lax.dot_general(a, b, (((0,), (0,)), ((), ())), preferred_element_type=F32)


def kernel(
    scale, gram_scale,
    design, small, sketch, gram,
    held, signs, table, arrived, partial, ring, code, owner, code_wide, pick,
    staged, slots, local, part_in, z_in,
    load_sem, ready, y_send, y_recv, z_send, z_recv, d_send, d_recv,
    a_send, a_recv, b_send, b_recv, c_send, c_recv,
):
    g = lax.axis_index("grp")
    dev = lax.axis_index("dev")
    z = dev // PEERS
    p = dev % PEERS
    holder = g * PEERS + p

    def holder_id(k):
        other = holder ^ k
        return (other // PEERS, z * PEERS + other % PEERS)

    loads = [
        pltpu.make_async_copy(
            design.at[:, pl.ds(i * 64, 64)], held.at[:, pl.ds(i * 64, 64)], load_sem.at[i]
        )
        for i in range(4)
    ]
    for load in loads:
        load.start()

    barrier = pltpu.get_barrier_semaphore()
    for k in range(1, PLANES):
        pl.semaphore_signal(barrier, inc=1, device_id=(g, z * PEERS + (p ^ k)), device_id_type=MESH)
        pl.semaphore_signal(barrier, inc=1, device_id=(g, (z ^ k) * PEERS + p), device_id_type=MESH)
    for k in range(1, GROUPS):
        pl.semaphore_signal(barrier, inc=1, device_id=(g ^ k, dev), device_id_type=MESH)

    lane = lax.broadcasted_iota(jnp.int32, (128, 128), 1)
    row = lax.broadcasted_iota(jnp.int32, (128, 128), 0)
    ones = jnp.ones((128, 128), BF16)
    for i in range(16):
        sign = (2 * small[pl.ds(BLOCKS + i, 1), :] - 1).astype(F32)
        diagonal = jnp.where(lane == row, jnp.broadcast_to(sign, (128, 128)), 0.0)
        signs[pl.ds(i * 128, 128), :] = dot(diagonal.astype(BF16), ones)

    target = small[pl.ds(0, BLOCKS), :]
    owner[...] = (target >> 5) & 63
    along_z = (target >> 14) & z
    flip = (along_z ^ (along_z >> 1) ^ (along_z >> 2)) & 1
    code[...] = ((((target >> 11) & 7) << 5) | (target & 31) | (flip << 8) | 512).astype(F32)

    for i in range(8):
        if i % 2 == 0:
            loads[i // 2].wait()
        rows_in = pl.ds(i * IN_RANGE, IN_RANGE)
        for half in range(2):
            cols = pl.ds(half * 128, 128)
            parts = [
                held[k, rows_in, cols] * signs[pl.ds(k * 256 + i * IN_RANGE, IN_RANGE), :]
                for k in range(8)
            ]
            for k, value in enumerate(butterfly(parts)):
                held[k, rows_in, cols] = value

    def y_copy(j, k):
        peer = p ^ k
        return pltpu.make_async_remote_copy(
            held.at[j, pl.ds(pl.multiple_of(peer * IN_RANGE, IN_RANGE), IN_RANGE)],
            arrived.at[j, pl.ds(pl.multiple_of(p * IN_RANGE, IN_RANGE), IN_RANGE)],
            y_send.at[j, k], y_recv.at[j, k],
            device_id=(g, z * PEERS + peer), device_id_type=MESH,
        )

    def y_landed(j, k):
        peer = p ^ k
        return pltpu.make_async_remote_copy(
            held.at[j, pl.ds(pl.multiple_of(p * IN_RANGE, IN_RANGE), IN_RANGE)],
            arrived.at[j, pl.ds(pl.multiple_of(peer * IN_RANGE, IN_RANGE), IN_RANGE)],
            y_send.at[j, k], y_recv.at[j, k],
            device_id=(g, z * PEERS + peer), device_id_type=MESH,
        )

    def low_bits(j, carry):
        for half in range(2):
            cols = pl.ds(half * 128, 128)
            parts = [held[j, pl.ds(k * IN_RANGE, IN_RANGE), cols] for k in range(8)]
            for k, value in enumerate(butterfly(parts)):
                held[j, pl.ds(k * IN_RANGE, IN_RANGE), cols] = value

        @pl.when(j == 0)
        def _():
            pl.semaphore_wait(barrier, PEERS - 1 + PLANES - 1 + GROUPS - 1)

        for k in (4, 5, 2, 3, 6, 7, 1):
            y_copy(j, k).start()
        mine = pl.multiple_of(p * IN_RANGE, IN_RANGE)
        arrived[j, pl.ds(mine, IN_RANGE), :] = held[j, pl.ds(mine, IN_RANGE), :]
        return carry

    lax.fori_loop(0, CHUNKS, low_bits, 0)

    for k in range(1, GROUPS):
        pl.semaphore_signal(ready, inc=1, device_id=(g ^ k, dev), device_id_type=MESH)

    before = (row < lane).astype(BF16)

    def build(j, carry):
        here = owner[...] == 8 * j + p
        rank = dot(here.astype(F32).astype(BF16), before)
        for i in range(SLOTS):
            chosen = jnp.where(here & (rank == float(i)), code[...], 0.0)
            column = jnp.sum(chosen, axis=1, keepdims=True)
            code_wide[pl.ds(i, BLOCKS, stride=SLOTS), :] = jnp.broadcast_to(column, (BLOCKS, 128))
        wide = code_wide[...].astype(jnp.int32)
        at = lax.broadcasted_iota(jnp.int32, (256, 128), 1) + 256
        for half in range(2):
            v = wide & (at + 128 * half)
            v = v ^ (v >> 8)
            v = v ^ (v >> 4)
            v = v ^ (v >> 2)
            v = v ^ (v >> 1)
            value = jnp.where(wide >= 512, 1 - 2 * (v & 1), 0).astype(F32)
            table[j, :, pl.ds(half * 128, 128)] = value.astype(BF16)
        return carry

    lax.fori_loop(0, CHUNKS, build, 0)

    own = jnp.broadcast_to((small[pl.ds(dev, 1), :] >> 5) & 63, (128, 128)).astype(F32)
    same = jnp.where((own == own.T) & (row < lane), 1.0, 0.0)
    rank = jnp.broadcast_to(jnp.sum(same, axis=0, keepdims=True), (128, 128))
    own = own.astype(jnp.int32)
    place = ((own & 7) * 32 + (own >> 3) * 4).astype(F32) + rank
    place = place.T
    for half in range(2):
        at = (lane + 128 * half).astype(F32)
        pick[:, pl.ds(half * 128, 128)] = jnp.where(place == at, 1.0, 0.0).astype(BF16)

    local[...] = jnp.zeros_like(local)

    def block(index):
        return pl.ds(pl.multiple_of(index * 32, 32), 32)

    def hop(j, way, step, source):
        step_z = 1 if way == 0 else PLANES - 1
        return pltpu.make_async_remote_copy(
            source, ring.at[j, way, step], z_send.at[j, way, step], z_recv.at[j, way, step],
            device_id=(g, (z + step_z) % PLANES * PEERS + p), device_id_type=MESH,
        )

    def reach(j, way):
        return 3 + (j + way + 1) % 2

    def dest(j, way, step):
        far = reach(j, way) - step
        return (z + far) % PLANES if way == 0 else (z + PLANES - far) % PLANES

    def produce(j):
        for k in range(1, PEERS):
            y_landed(j, k).wait_recv()
        high, low = split2(arrived[j])
        partial[j] = dot(table[j], high) + dot(table[j], low)
        for way in range(2):
            hop(j, way, 0, partial.at[j, block(dest(j, way, 0))]).start()

    def deliver(m, k):
        peer = p ^ k
        return pltpu.make_async_remote_copy(
            staged.at[m, peer], slots.at[pl.ds(pl.multiple_of(p * 32 + m * 8, 8), 8)],
            d_send.at[m, k], d_recv.at[m, k],
            device_id=(g, z * PEERS + peer), device_id_type=MESH,
        )

    def delivered(m, k):
        peer = p ^ k
        return pltpu.make_async_remote_copy(
            staged.at[m, p], slots.at[pl.ds(pl.multiple_of(peer * 32 + m * 8, 8), 8)],
            d_send.at[m, k], d_recv.at[m, k],
            device_id=(g, z * PEERS + peer), device_id_type=MESH,
        )

    def send_pair(m):
        for k in (4, 5, 2, 3, 6, 7, 1):
            deliver(m, k).start()
        slots[pl.ds(pl.multiple_of(p * 32 + m * 8, 8), 8), :] = staged[m, p]

    def forward(j, step):
        for way in range(2):
            def take(way=way):
                hop(j, way, step - 1, partial.at[j, block(0)]).wait_recv()

            def send(way=way):
                ring[j, way, step - 1] += partial[j, block(dest(j, way, step)), :]
                hop(j, way, step, ring.at[j, way, step - 1]).start()

            if step <= 2:
                take()
                send()
            elif step == 3:
                take()
                pl.when(reach(j, way) == 4)(send)
            else:
                pl.when(reach(j, way) == 4)(take)

    def finish(j):
        done = partial[j, block(z), :]
        for way in range(2):
            done = done + ring[j, way, reach(j, way) - 1]
        m = j // 2
        for odd in range(2):

            @pl.when(j % 2 == odd)
            def _(odd=odd):
                for k in range(PEERS):
                    staged[m, k, pl.ds(odd * SLOTS, SLOTS), :] = done[k * SLOTS : (k + 1) * SLOTS, :]

        high, low = split2(done)
        local[...] += dot_first(high, high) + dot_first(high, low) + dot_first(low, high)

        @pl.when((j % 2 == 1) & (j < CHUNKS - 1))
        def _():
            send_pair(m)

    def turn(t, carry):
        @pl.when(t < CHUNKS)
        def _():
            produce(t)

        for step in range(1, 5):
            j = t - LAG * step

            @pl.when((j >= 0) & (j < CHUNKS))
            def _(j=j, step=step):
                forward(j, step)
                if step == 4:
                    finish(j)

        return carry

    lax.fori_loop(0, CHUNKS + 4 * LAG, turn, 0)

    def rows(index):
        return pl.ds(pl.multiple_of(index * 8, 8), 8)

    def copy_a(k):
        return pltpu.make_async_remote_copy(
            local.at[rows(holder ^ k)], part_in.at[rows(holder)], a_send, a_recv,
            device_id=holder_id(k), device_id_type=MESH,
        )

    def copy_b(k):
        return pltpu.make_async_remote_copy(
            z_in.at[rows(z)], z_in.at[rows(z)], b_send, b_recv,
            device_id=(g, (z ^ k) * PEERS + p), device_id_type=MESH,
        )

    def copy_c(k):
        return pltpu.make_async_remote_copy(
            gram.at[rows(holder)], gram.at[rows(holder)], c_send, c_recv,
            device_id=holder_id(k), device_id_type=MESH,
        )

    def wait_all(ref, count, sem):
        whole = ref.at[pl.ds(0, count * 8)]
        pltpu.make_async_copy(whole, whole, sem).wait()

    pl.semaphore_wait(ready, GROUPS - 1)
    for k in FAR_FIRST:
        copy_a(k).start()
    part_in[rows(holder), :] = local[rows(holder), :]
    send_pair(CHUNKS // 2 - 1)

    def gone(j, carry):
        for k in range(1, PEERS):
            y_copy(j, k).wait_send()
        for way in range(2):
            for step in range(3):
                hop(j, way, step, ring.at[j, way, step]).wait_send()

            @pl.when(reach(j, way) == 4)
            def _(way=way):
                hop(j, way, 3, ring.at[j, way, 2]).wait_send()
        return carry

    lax.fori_loop(0, CHUNKS, gone, 0)

    for m in range(CHUNKS // 2):
        for k in range(1, PEERS):
            delivered(m, k).wait_recv()
            deliver(m, k).wait_send()
    value = slots[...]
    first, rest = split2(value)
    second, third = split2(value - first.astype(F32))
    sketch[...] = (dot(pick[...], first) + dot(pick[...], second) + dot(pick[...], third)) * scale

    wait_all(part_in, HOLDERS - 1, a_recv)
    z_in[rows(z), :] = jnp.sum(part_in[...].reshape(HOLDERS, 8, 256), axis=0)
    for k in (4, 3, 5, 2, 6, 1, 7):
        copy_b(k).start()
    wait_all(part_in, HOLDERS - 1, a_send)
    wait_all(z_in, PLANES - 1, b_recv)
    gram[rows(holder), :] = jnp.sum(z_in[...].reshape(PLANES, 8, 256), axis=0) * gram_scale
    for k in FAR_FIRST:
        copy_c(k).start()
    wait_all(z_in, PLANES - 1, b_send)
    wait_all(gram, HOLDERS - 1, c_recv)
    wait_all(gram, HOLDERS - 1, c_send)


def shards(design, sign_bits, sample_rows):
    rows, width = design.shape
    slab = rows * lax.axis_size("dev")
    total = lax.axis_size("grp") * sample_rows.shape[1]
    vmem = pl.BlockSpec(memory_space=pltpu.VMEM)
    small = jnp.concatenate([sample_rows.reshape(BLOCKS, 128), sign_bits.reshape(16, 128)])
    dma = pltpu.SemaphoreType.DMA
    return pl.pallas_call(
        functools.partial(kernel, 1.0 / math.sqrt(slab), 1.0 / (slab * total)),
        out_shape=(
            jax.ShapeDtypeStruct((128, width), F32),
            jax.ShapeDtypeStruct((width, width), F32),
        ),
        in_specs=[pl.BlockSpec(memory_space=pltpu.HBM), vmem],
        out_specs=(vmem, vmem),
        scratch_shapes=[
            pltpu.VMEM((CHUNKS, 256, 256), F32),
            pltpu.VMEM((2048, 128), F32),
            pltpu.VMEM((CHUNKS, 256, 256), BF16),
            pltpu.VMEM((CHUNKS, 256, 256), F32),
            pltpu.VMEM((CHUNKS, 256, 256), F32),
            pltpu.VMEM((CHUNKS, 2, 4, 32, 256), F32),
            pltpu.VMEM((BLOCKS, 128), F32),
            pltpu.VMEM((BLOCKS, 128), jnp.int32),
            pltpu.VMEM((256, 128), F32),
            pltpu.VMEM((128, 256), BF16),
            pltpu.VMEM((CHUNKS // 2, PEERS, 8, 256), F32),
            pltpu.VMEM((256, 256), F32),
            pltpu.VMEM((256, 256), F32),
            pltpu.VMEM((HOLDERS * 8, 256), F32),
            pltpu.VMEM((PLANES * 8, 256), F32),
            dma((4,)),
            pltpu.SemaphoreType.REGULAR,
            dma((CHUNKS, PEERS)), dma((CHUNKS, PEERS)),
            dma((CHUNKS, 2, 4)), dma((CHUNKS, 2, 4)),
            dma((CHUNKS // 2, PEERS)), dma((CHUNKS // 2, PEERS)),
            dma, dma, dma, dma, dma, dma,
        ],
        compiler_params=pltpu.CompilerParams(
            collective_id=0, has_side_effects=True, vmem_limit_bytes=52 << 20
        ),
        cost_estimate=pl.CostEstimate(flops=2 * 10**9, bytes_accessed=4 << 20, transcendentals=0),
    )(design.reshape(CHUNKS, 256, width), small)


def solution(mesh):
    return jax.shard_map(
        shards,
        mesh=mesh,
        in_specs=(P(("grp", "dev"), None), P(("grp", "dev")), P("grp", None)),
        out_specs=(P(("grp", "dev"), None), P()),
        check_vma=False,
    )
```

```python
import functools
import math

import jax
import jax.numpy as jnp
from jax import lax
from jax.experimental import pallas as pl
from jax.experimental.pallas import tpu as pltpu
from jax.sharding import PartitionSpec as P

MESH = pl.DeviceIdType.MESH
F32 = jnp.float32
BF16 = jnp.bfloat16

GROUPS = 4
PLANES = 8
PEERS = 8
CHUNKS = 8
IN_RANGE = 32
SLOTS = 4
BLOCKS = 64
HOLDERS = 32
FAR_FIRST = tuple(k ^ 20 for k in range(HOLDERS) if k != 20)
LAG = 2


def butterfly(parts):
    span = 1
    while span < len(parts):
        out = list(parts)
        for a in range(len(parts)):
            if a & span == 0:
                out[a] = parts[a] + parts[a + span]
                out[a + span] = parts[a] - parts[a + span]
        parts = out
        span *= 2
    return parts


def split2(value):
    high = value.astype(BF16)
    return high, (value - high.astype(F32)).astype(BF16)


def dot(a, b):
    return jnp.dot(a, b, preferred_element_type=F32)


def dot_first(a, b):
    return lax.dot_general(a, b, (((0,), (0,)), ((), ())), preferred_element_type=F32)


def kernel(
    scale, gram_scale,
    design, small, sketch, gram,
    held, signs, table, arrived, partial, ring, code, owner, code_wide, pick,
    staged, slots, local, part_in, z_in,
    load_sem, ready, y_send, y_recv, z_send, z_recv, d_send, d_recv,
    a_send, a_recv, b_send, b_recv, c_send, c_recv,
):
    g = lax.axis_index("grp")
    dev = lax.axis_index("dev")
    z = dev // PEERS
    p = dev % PEERS
    holder = g * PEERS + p

    def holder_id(k):
        other = holder ^ k
        return (other // PEERS, z * PEERS + other % PEERS)

    loads = [
        pltpu.make_async_copy(
            design.at[:, pl.ds(i * 64, 64)], held.at[:, pl.ds(i * 64, 64)], load_sem.at[i]
        )
        for i in range(4)
    ]
    for load in loads:
        load.start()

    barrier = pltpu.get_barrier_semaphore()
    for k in range(1, PLANES):
        pl.semaphore_signal(barrier, inc=1, device_id=(g, z * PEERS + (p ^ k)), device_id_type=MESH)
        pl.semaphore_signal(barrier, inc=1, device_id=(g, (z ^ k) * PEERS + p), device_id_type=MESH)
    for k in range(1, GROUPS):
        pl.semaphore_signal(barrier, inc=1, device_id=(g ^ k, dev), device_id_type=MESH)

    lane = lax.broadcasted_iota(jnp.int32, (128, 128), 1)
    row = lax.broadcasted_iota(jnp.int32, (128, 128), 0)
    ones = jnp.ones((128, 128), BF16)
    for i in range(16):
        sign = (2 * small[pl.ds(BLOCKS + i, 1), :] - 1).astype(F32)
        diagonal = jnp.where(lane == row, jnp.broadcast_to(sign, (128, 128)), 0.0)
        signs[pl.ds(i * 128, 128), :] = dot(diagonal.astype(BF16), ones)

    target = small[pl.ds(0, BLOCKS), :]
    owner[...] = (target >> 5) & 63
    along_z = (target >> 14) & z
    flip = (along_z ^ (along_z >> 1) ^ (along_z >> 2)) & 1
    code[...] = ((((target >> 11) & 7) << 5) | (target & 31) | (flip << 8) | 512).astype(F32)

    for i in range(8):
        if i % 2 == 0:
            loads[i // 2].wait()
        rows_in = pl.ds(i * IN_RANGE, IN_RANGE)
        for half in range(2):
            cols = pl.ds(half * 128, 128)
            parts = [
                held[k, rows_in, cols] * signs[pl.ds(k * 256 + i * IN_RANGE, IN_RANGE), :]
                for k in range(8)
            ]
            for k, value in enumerate(butterfly(parts)):
                held[k, rows_in, cols] = value

    def y_copy(j, k):
        peer = p ^ k
        return pltpu.make_async_remote_copy(
            held.at[j, pl.ds(pl.multiple_of(peer * IN_RANGE, IN_RANGE), IN_RANGE)],
            arrived.at[j, pl.ds(pl.multiple_of(p * IN_RANGE, IN_RANGE), IN_RANGE)],
            y_send, y_recv.at[j],
            device_id=(g, z * PEERS + peer), device_id_type=MESH,
        )

    def wait_bytes(ref, sem):
        pltpu.make_async_copy(ref, ref, sem).wait()

    def low_bits(j, carry):
        for half in range(2):
            cols = pl.ds(half * 128, 128)
            parts = [held[j, pl.ds(k * IN_RANGE, IN_RANGE), cols] for k in range(8)]
            for k, value in enumerate(butterfly(parts)):
                held[j, pl.ds(k * IN_RANGE, IN_RANGE), cols] = value

        @pl.when(j == 0)
        def _():
            pl.semaphore_wait(barrier, PEERS - 1 + PLANES - 1 + GROUPS - 1)

        for k in (4, 5, 2, 3, 6, 7, 1):
            y_copy(j, k).start()
        mine = pl.multiple_of(p * IN_RANGE, IN_RANGE)
        arrived[j, pl.ds(mine, IN_RANGE), :] = held[j, pl.ds(mine, IN_RANGE), :]
        return carry

    lax.fori_loop(0, CHUNKS, low_bits, 0)

    for k in range(1, GROUPS):
        pl.semaphore_signal(ready, inc=1, device_id=(g ^ k, dev), device_id_type=MESH)

    before = (row < lane).astype(BF16)

    def build(j, carry):
        here = owner[...] == 8 * j + p
        rank = dot(here.astype(F32).astype(BF16), before)
        for i in range(SLOTS):
            chosen = jnp.where(here & (rank == float(i)), code[...], 0.0)
            column = jnp.sum(chosen, axis=1, keepdims=True)
            code_wide[pl.ds(i, BLOCKS, stride=SLOTS), :] = jnp.broadcast_to(column, (BLOCKS, 128))
        wide = code_wide[...].astype(jnp.int32)
        at = lax.broadcasted_iota(jnp.int32, (256, 128), 1) + 256
        for half in range(2):
            v = wide & (at + 128 * half)
            v = v ^ (v >> 8)
            v = v ^ (v >> 4)
            v = v ^ (v >> 2)
            v = v ^ (v >> 1)
            value = jnp.where(wide >= 512, 1 - 2 * (v & 1), 0).astype(F32)
            table[j, :, pl.ds(half * 128, 128)] = value.astype(BF16)
        return carry

    lax.fori_loop(0, CHUNKS, build, 0)

    own = jnp.broadcast_to((small[pl.ds(dev, 1), :] >> 5) & 63, (128, 128)).astype(F32)
    same = jnp.where((own == own.T) & (row < lane), 1.0, 0.0)
    rank = jnp.broadcast_to(jnp.sum(same, axis=0, keepdims=True), (128, 128))
    own = own.astype(jnp.int32)
    place = ((own & 7) * 32 + (own >> 3) * 4).astype(F32) + rank
    place = place.T
    for half in range(2):
        at = (lane + 128 * half).astype(F32)
        pick[:, pl.ds(half * 128, 128)] = jnp.where(place == at, 1.0, 0.0).astype(BF16)

    local[...] = jnp.zeros_like(local)

    def block(index):
        return pl.ds(pl.multiple_of(index * 32, 32), 32)

    def hop(j, way, step, source):
        step_z = 1 if way == 0 else PLANES - 1
        return pltpu.make_async_remote_copy(
            source, ring.at[j, step, way], z_send, z_recv.at[j, step],
            device_id=(g, (z + step_z) % PLANES * PEERS + p), device_id_type=MESH,
        )

    def reach(j, way):
        return 3 + (j + way + 1) % 2

    def dest(j, way, step):
        far = reach(j, way) - step
        return (z + far) % PLANES if way == 0 else (z + PLANES - far) % PLANES

    def produce(j):
        wait_bytes(arrived.at[j, pl.ds(0, (PEERS - 1) * IN_RANGE)], y_recv.at[j])
        high, low = split2(arrived[j])
        partial[j] = dot(table[j], high) + dot(table[j], low)
        for way in range(2):
            hop(j, way, 0, partial.at[j, block(dest(j, way, 0))]).start()

    def deliver(m, k):
        peer = p ^ k
        return pltpu.make_async_remote_copy(
            staged.at[m, peer], slots.at[pl.ds(pl.multiple_of(p * 32 + m * 8, 8), 8)],
            d_send, d_recv,
            device_id=(g, z * PEERS + peer), device_id_type=MESH,
        )

    def send_pair(m):
        for k in (4, 5, 2, 3, 6, 7, 1):
            deliver(m, k).start()
        slots[pl.ds(pl.multiple_of(p * 32 + m * 8, 8), 8), :] = staged[m, p]

    def forward(j, step):
        if step < 4:
            wait_bytes(ring.at[j, step - 1], z_recv.at[j, step - 1])
        else:
            wait_bytes(ring.at[j, 3, 0], z_recv.at[j, 3])
        for way in range(2):
            def send(way=way):
                ring[j, step - 1, way] += partial[j, block(dest(j, way, step)), :]
                hop(j, way, step, ring.at[j, step - 1, way]).start()

            if step <= 2:
                send()
            elif step == 3:
                pl.when(reach(j, way) == 4)(send)

    def finish(j):
        done = partial[j, block(z), :]
        for way in range(2):
            done = done + ring[j, reach(j, way) - 1, way]
        m = j // 2
        for odd in range(2):

            @pl.when(j % 2 == odd)
            def _(odd=odd):
                for k in range(PEERS):
                    staged[m, k, pl.ds(odd * SLOTS, SLOTS), :] = done[k * SLOTS : (k + 1) * SLOTS, :]

        high, low = split2(done)
        local[...] += dot_first(high, high) + dot_first(high, low) + dot_first(low, high)

        @pl.when((j % 2 == 1) & (j < CHUNKS - 1))
        def _():
            send_pair(m)

    def turn(t, carry):
        @pl.when(t < CHUNKS)
        def _():
            produce(t)

        for step in range(1, 5):
            j = t - LAG * step

            @pl.when((j >= 0) & (j < CHUNKS))
            def _(j=j, step=step):
                forward(j, step)
                if step == 4:
                    finish(j)

        return carry

    lax.fori_loop(0, CHUNKS + 4 * LAG, turn, 0)

    def rows(index):
        return pl.ds(pl.multiple_of(index * 8, 8), 8)

    def copy_a(k):
        return pltpu.make_async_remote_copy(
            local.at[rows(holder ^ k)], part_in.at[rows(holder)], a_send, a_recv,
            device_id=holder_id(k), device_id_type=MESH,
        )

    def copy_b(k):
        return pltpu.make_async_remote_copy(
            z_in.at[rows(z)], z_in.at[rows(z)], b_send, b_recv,
            device_id=(g, (z ^ k) * PEERS + p), device_id_type=MESH,
        )

    def copy_c(k):
        return pltpu.make_async_remote_copy(
            gram.at[rows(holder)], gram.at[rows(holder)], c_send, c_recv,
            device_id=holder_id(k), device_id_type=MESH,
        )

    def wait_all(ref, count, sem):
        wait_bytes(ref.at[pl.ds(0, count * 8)], sem)

    pl.semaphore_wait(ready, GROUPS - 1)
    for k in FAR_FIRST:
        copy_a(k).start()
    part_in[rows(holder), :] = local[rows(holder), :]
    send_pair(CHUNKS // 2 - 1)

    wait_bytes(held.at[pl.ds(0, PEERS - 1)], y_send)
    wait_bytes(partial.at[pl.ds(0, PLANES - 1)], z_send)

    wait_bytes(slots.at[pl.ds(0, (PEERS - 1) * 32)], d_recv)
    wait_bytes(slots.at[pl.ds(0, (PEERS - 1) * 32)], d_send)
    value = slots[...]
    first, rest = split2(value)
    second, third = split2(value - first.astype(F32))
    sketch[...] = (dot(pick[...], first) + dot(pick[...], second) + dot(pick[...], third)) * scale

    wait_all(part_in, HOLDERS - 1, a_recv)
    z_in[rows(z), :] = jnp.sum(part_in[...].reshape(HOLDERS, 8, 256), axis=0)
    for k in (4, 3, 5, 2, 6, 1, 7):
        copy_b(k).start()
    wait_all(part_in, HOLDERS - 1, a_send)
    wait_all(z_in, PLANES - 1, b_recv)
    gram[rows(holder), :] = jnp.sum(z_in[...].reshape(PLANES, 8, 256), axis=0) * gram_scale
    for k in FAR_FIRST:
        copy_c(k).start()
    wait_all(z_in, PLANES - 1, b_send)
    wait_all(gram, HOLDERS - 1, c_recv)
    wait_all(gram, HOLDERS - 1, c_send)


def shards(design, sign_bits, sample_rows):
    rows, width = design.shape
    slab = rows * lax.axis_size("dev")
    total = lax.axis_size("grp") * sample_rows.shape[1]
    vmem = pl.BlockSpec(memory_space=pltpu.VMEM)
    small = jnp.concatenate([sample_rows.reshape(BLOCKS, 128), sign_bits.reshape(16, 128)])
    dma = pltpu.SemaphoreType.DMA
    return pl.pallas_call(
        functools.partial(kernel, 1.0 / math.sqrt(slab), 1.0 / (slab * total)),
        out_shape=(
            jax.ShapeDtypeStruct((128, width), F32),
            jax.ShapeDtypeStruct((width, width), F32),
        ),
        in_specs=[pl.BlockSpec(memory_space=pltpu.HBM), vmem],
        out_specs=(vmem, vmem),
        scratch_shapes=[
            pltpu.VMEM((CHUNKS, 256, 256), F32),
            pltpu.VMEM((2048, 128), F32),
            pltpu.VMEM((CHUNKS, 256, 256), BF16),
            pltpu.VMEM((CHUNKS, 256, 256), F32),
            pltpu.VMEM((CHUNKS, 256, 256), F32),
            pltpu.VMEM((CHUNKS, 4, 2, 32, 256), F32),
            pltpu.VMEM((BLOCKS, 128), F32),
            pltpu.VMEM((BLOCKS, 128), jnp.int32),
            pltpu.VMEM((256, 128), F32),
            pltpu.VMEM((128, 256), BF16),
            pltpu.VMEM((CHUNKS // 2, PEERS, 8, 256), F32),
            pltpu.VMEM((256, 256), F32),
            pltpu.VMEM((256, 256), F32),
            pltpu.VMEM((HOLDERS * 8, 256), F32),
            pltpu.VMEM((PLANES * 8, 256), F32),
            dma((4,)),
            pltpu.SemaphoreType.REGULAR,
            dma, dma((CHUNKS,)),
            dma, dma((CHUNKS, 4)),
            dma, dma,
            dma, dma, dma, dma, dma, dma,
        ],
        compiler_params=pltpu.CompilerParams(
            collective_id=0, has_side_effects=True, vmem_limit_bytes=52 << 20
        ),
        cost_estimate=pl.CostEstimate(flops=2 * 10**9, bytes_accessed=4 << 20, transcendentals=0),
    )(design.reshape(CHUNKS, 256, width), small)


def solution(mesh):
    return jax.shard_map(
        shards,
        mesh=mesh,
        in_specs=(P(("grp", "dev"), None), P(("grp", "dev")), P("grp", None)),
        out_specs=(P(("grp", "dev"), None), P()),
        check_vma=False,
    )
```

```python
import functools
import math

import jax
import jax.numpy as jnp
from jax import lax
from jax.experimental import pallas as pl
from jax.experimental.pallas import tpu as pltpu
from jax.sharding import PartitionSpec as P

MESH = pl.DeviceIdType.MESH
F32 = jnp.float32
BF16 = jnp.bfloat16

GROUPS = 4
PLANES = 8
PEERS = 8
CHUNKS = 8
IN_RANGE = 32
SLOTS = 4
BLOCKS = 64
HOLDERS = 32
FAR_FIRST = tuple(k ^ 20 for k in range(HOLDERS) if k != 20)
LAG = 2


def butterfly(parts):
    span = 1
    while span < len(parts):
        out = list(parts)
        for a in range(len(parts)):
            if a & span == 0:
                out[a] = parts[a] + parts[a + span]
                out[a + span] = parts[a] - parts[a + span]
        parts = out
        span *= 2
    return parts


def split2(value):
    high = value.astype(BF16)
    return high, (value - high.astype(F32)).astype(BF16)


def dot(a, b):
    return jnp.dot(a, b, preferred_element_type=F32)


def dot_first(a, b):
    return lax.dot_general(a, b, (((0,), (0,)), ((), ())), preferred_element_type=F32)


def kernel(
    scale, gram_scale,
    design, small, sketch, gram,
    held, signs, table, arrived, partial, ring, code, owner, code_wide, pick,
    staged, slots, local, part_in, z_in,
    load_sem, ready, y_send, y_recv, z_send, z_recv, d_send, d_recv,
    a_send, a_recv, b_send, b_recv, c_send, c_recv,
):
    g = lax.axis_index("grp")
    dev = lax.axis_index("dev")
    z = dev // PEERS
    p = dev % PEERS
    holder = g * PEERS + p

    def holder_id(k):
        other = holder ^ k
        return (other // PEERS, z * PEERS + other % PEERS)

    loads = [
        pltpu.make_async_copy(
            design.at[:, pl.ds(i * 64, 64)], held.at[:, pl.ds(i * 64, 64)], load_sem.at[i]
        )
        for i in range(4)
    ]
    for load in loads:
        load.start()

    z_next = [(g, (z + k) % PLANES * PEERS + p) for k in (1, PLANES - 1)]
    x_next = [((g + k) % GROUPS, dev) for k in (1, GROUPS - 1)]
    barrier = pltpu.get_barrier_semaphore()
    for peer in [(g, z * PEERS + (p ^ k)) for k in (4, 5, 2, 3, 6, 7, 1)] + z_next + x_next:
        pl.semaphore_signal(barrier, inc=1, device_id=peer, device_id_type=MESH)

    lane = lax.broadcasted_iota(jnp.int32, (128, 128), 1)
    row = lax.broadcasted_iota(jnp.int32, (128, 128), 0)
    ones = jnp.ones((128, 128), BF16)
    for i in range(16):
        sign = (2 * small[pl.ds(BLOCKS + i, 1), :] - 1).astype(F32)
        diagonal = jnp.where(lane == row, jnp.broadcast_to(sign, (128, 128)), 0.0)
        signs[pl.ds(i * 128, 128), :] = dot(diagonal.astype(BF16), ones)

    target = small[pl.ds(0, BLOCKS), :]
    owner[...] = (target >> 5) & 63
    along_z = (target >> 14) & z
    flip = (along_z ^ (along_z >> 1) ^ (along_z >> 2)) & 1
    code[...] = ((((target >> 11) & 7) << 5) | (target & 31) | (flip << 8) | 512).astype(F32)

    for i in range(8):
        if i % 2 == 0:
            loads[i // 2].wait()
        rows_in = pl.ds(i * IN_RANGE, IN_RANGE)
        for half in range(2):
            cols = pl.ds(half * 128, 128)
            parts = [
                held[k, rows_in, cols] * signs[pl.ds(k * 256 + i * IN_RANGE, IN_RANGE), :]
                for k in range(8)
            ]
            for k, value in enumerate(butterfly(parts)):
                held[k, rows_in, cols] = value

    def y_copy(j, k):
        peer = p ^ k
        return pltpu.make_async_remote_copy(
            held.at[j, pl.ds(pl.multiple_of(peer * IN_RANGE, IN_RANGE), IN_RANGE)],
            arrived.at[j, pl.ds(pl.multiple_of(p * IN_RANGE, IN_RANGE), IN_RANGE)],
            y_send, y_recv.at[j],
            device_id=(g, z * PEERS + peer), device_id_type=MESH,
        )

    def wait_bytes(ref, sem):
        pltpu.make_async_copy(ref, ref, sem).wait()

    def low_bits(j, carry):
        for half in range(2):
            cols = pl.ds(half * 128, 128)
            parts = [held[j, pl.ds(k * IN_RANGE, IN_RANGE), cols] for k in range(8)]
            for k, value in enumerate(butterfly(parts)):
                held[j, pl.ds(k * IN_RANGE, IN_RANGE), cols] = value

        @pl.when(j == 0)
        def _():
            pl.semaphore_wait(barrier, PEERS - 1 + 2 + 2)

        for k in (4, 5, 2, 3, 6, 7, 1):
            y_copy(j, k).start()
        mine = pl.multiple_of(p * IN_RANGE, IN_RANGE)
        arrived[j, pl.ds(mine, IN_RANGE), :] = held[j, pl.ds(mine, IN_RANGE), :]
        return carry

    lax.fori_loop(0, CHUNKS, low_bits, 0)

    for stage in range(2):
        for peer in x_next:
            pl.semaphore_signal(ready.at[stage], inc=1, device_id=peer, device_id_type=MESH)
        if stage == 0:
            pl.semaphore_wait(ready.at[0], 2)

    before = (row < lane).astype(BF16)

    def build(j, carry):
        here = owner[...] == 8 * j + p
        rank = dot(here.astype(F32).astype(BF16), before)
        for i in range(SLOTS):
            chosen = jnp.where(here & (rank == float(i)), code[...], 0.0)
            column = jnp.sum(chosen, axis=1, keepdims=True)
            code_wide[pl.ds(i, BLOCKS, stride=SLOTS), :] = jnp.broadcast_to(column, (BLOCKS, 128))
        wide = code_wide[...].astype(jnp.int32)
        at = lax.broadcasted_iota(jnp.int32, (256, 128), 1) + 256
        for half in range(2):
            v = wide & (at + 128 * half)
            v = v ^ (v >> 8)
            v = v ^ (v >> 4)
            v = v ^ (v >> 2)
            v = v ^ (v >> 1)
            value = jnp.where(wide >= 512, 1 - 2 * (v & 1), 0).astype(F32)
            table[j, :, pl.ds(half * 128, 128)] = value.astype(BF16)
        return carry

    lax.fori_loop(0, CHUNKS, build, 0)

    own = jnp.broadcast_to((small[pl.ds(dev, 1), :] >> 5) & 63, (128, 128)).astype(F32)
    same = jnp.where((own == own.T) & (row < lane), 1.0, 0.0)
    rank = jnp.broadcast_to(jnp.sum(same, axis=0, keepdims=True), (128, 128))
    own = own.astype(jnp.int32)
    place = ((own & 7) * 32 + (own >> 3) * 4).astype(F32) + rank
    place = place.T
    for half in range(2):
        at = (lane + 128 * half).astype(F32)
        pick[:, pl.ds(half * 128, 128)] = jnp.where(place == at, 1.0, 0.0).astype(BF16)

    local[...] = jnp.zeros_like(local)

    def block(index):
        return pl.ds(pl.multiple_of(index * 32, 32), 32)

    def hop(j, way, step, source):
        step_z = 1 if way == 0 else PLANES - 1
        return pltpu.make_async_remote_copy(
            source, ring.at[j, step, way], z_send, z_recv.at[j, step],
            device_id=(g, (z + step_z) % PLANES * PEERS + p), device_id_type=MESH,
        )

    def reach(j, way):
        return 3 + (j + way + 1) % 2

    def dest(j, way, step):
        far = reach(j, way) - step
        return (z + far) % PLANES if way == 0 else (z + PLANES - far) % PLANES

    def produce(j):
        wait_bytes(arrived.at[j, pl.ds(0, (PEERS - 1) * IN_RANGE)], y_recv.at[j])
        high, low = split2(arrived[j])
        partial[j] = dot(table[j], high) + dot(table[j], low)
        for way in range(2):
            hop(j, way, 0, partial.at[j, block(dest(j, way, 0))]).start()

    def deliver(m, k):
        peer = p ^ k
        return pltpu.make_async_remote_copy(
            staged.at[m, peer], slots.at[pl.ds(pl.multiple_of(p * 32 + m * 8, 8), 8)],
            d_send, d_recv,
            device_id=(g, z * PEERS + peer), device_id_type=MESH,
        )

    def send_pair(m):
        for k in (4, 5, 2, 3, 6, 7, 1):
            deliver(m, k).start()
        slots[pl.ds(pl.multiple_of(p * 32 + m * 8, 8), 8), :] = staged[m, p]

    def forward(j, step):
        if step < 4:
            wait_bytes(ring.at[j, step - 1], z_recv.at[j, step - 1])
        else:
            wait_bytes(ring.at[j, 3, 0], z_recv.at[j, 3])
        for way in range(2):
            def send(way=way):
                ring[j, step - 1, way] += partial[j, block(dest(j, way, step)), :]
                hop(j, way, step, ring.at[j, step - 1, way]).start()

            if step <= 2:
                send()
            elif step == 3:
                pl.when(reach(j, way) == 4)(send)

    def finish(j):
        done = partial[j, block(z), :]
        for way in range(2):
            done = done + ring[j, reach(j, way) - 1, way]
        m = j // 2
        for odd in range(2):

            @pl.when(j % 2 == odd)
            def _(odd=odd):
                for k in range(PEERS):
                    staged[m, k, pl.ds(odd * SLOTS, SLOTS), :] = done[k * SLOTS : (k + 1) * SLOTS, :]

        high, low = split2(done)
        local[...] += dot_first(high, high) + dot_first(high, low) + dot_first(low, high)

        @pl.when((j % 2 == 1) & (j < CHUNKS - 1))
        def _():
            send_pair(m)

    def turn(t, carry):
        for step in range(1, 5):
            j = t - LAG * step

            @pl.when((j >= 0) & (j < CHUNKS))
            def _(j=j, step=step):
                forward(j, step)
                if step == 4:
                    finish(j)

        @pl.when(t < CHUNKS)
        def _():
            produce(t)

        return carry

    lax.fori_loop(0, CHUNKS + 4 * LAG, turn, 0)

    def rows(index):
        return pl.ds(pl.multiple_of(index * 8, 8), 8)

    def copy_a(k):
        return pltpu.make_async_remote_copy(
            local.at[rows(holder ^ k)], part_in.at[rows(holder)], a_send, a_recv,
            device_id=holder_id(k), device_id_type=MESH,
        )

    def copy_b(k):
        return pltpu.make_async_remote_copy(
            z_in.at[rows(z)], z_in.at[rows(z)], b_send, b_recv,
            device_id=(g, (z ^ k) * PEERS + p), device_id_type=MESH,
        )

    def copy_c(k):
        return pltpu.make_async_remote_copy(
            gram.at[rows(holder)], gram.at[rows(holder)], c_send, c_recv,
            device_id=holder_id(k), device_id_type=MESH,
        )

    def wait_all(ref, count, sem):
        wait_bytes(ref.at[pl.ds(0, count * 8)], sem)

    pl.semaphore_wait(ready.at[1], 2)
    for k in FAR_FIRST:
        copy_a(k).start()
    part_in[rows(holder), :] = local[rows(holder), :]
    send_pair(CHUNKS // 2 - 1)

    wait_bytes(held.at[pl.ds(0, PEERS - 1)], y_send)
    wait_bytes(partial.at[pl.ds(0, PLANES - 1)], z_send)

    wait_bytes(slots.at[pl.ds(0, (PEERS - 1) * 32)], d_recv)
    wait_bytes(slots.at[pl.ds(0, (PEERS - 1) * 32)], d_send)
    value = slots[...]
    first, rest = split2(value)
    second, third = split2(value - first.astype(F32))
    sketch[...] = (dot(pick[...], first) + dot(pick[...], second) + dot(pick[...], third)) * scale

    wait_all(part_in, HOLDERS - 1, a_recv)
    z_in[rows(z), :] = jnp.sum(part_in[...].reshape(HOLDERS, 8, 256), axis=0)
    for k in (4, 3, 5, 2, 6, 1, 7):
        copy_b(k).start()
    wait_all(part_in, HOLDERS - 1, a_send)
    wait_all(z_in, PLANES - 1, b_recv)
    gram[rows(holder), :] = jnp.sum(z_in[...].reshape(PLANES, 8, 256), axis=0) * gram_scale
    for k in FAR_FIRST:
        copy_c(k).start()
    wait_all(z_in, PLANES - 1, b_send)
    wait_all(gram, HOLDERS - 1, c_recv)
    wait_all(gram, HOLDERS - 1, c_send)


def shards(design, sign_bits, sample_rows):
    rows, width = design.shape
    slab = rows * lax.axis_size("dev")
    total = lax.axis_size("grp") * sample_rows.shape[1]
    vmem = pl.BlockSpec(memory_space=pltpu.VMEM)
    small = jnp.concatenate([sample_rows.reshape(BLOCKS, 128), sign_bits.reshape(16, 128)])
    dma = pltpu.SemaphoreType.DMA
    return pl.pallas_call(
        functools.partial(kernel, 1.0 / math.sqrt(slab), 1.0 / (slab * total)),
        out_shape=(
            jax.ShapeDtypeStruct((128, width), F32),
            jax.ShapeDtypeStruct((width, width), F32),
        ),
        in_specs=[pl.BlockSpec(memory_space=pltpu.HBM), vmem],
        out_specs=(vmem, vmem),
        scratch_shapes=[
            pltpu.VMEM((CHUNKS, 256, 256), F32),
            pltpu.VMEM((2048, 128), F32),
            pltpu.VMEM((CHUNKS, 256, 256), BF16),
            pltpu.VMEM((CHUNKS, 256, 256), F32),
            pltpu.VMEM((CHUNKS, 256, 256), F32),
            pltpu.VMEM((CHUNKS, 4, 2, 32, 256), F32),
            pltpu.VMEM((BLOCKS, 128), F32),
            pltpu.VMEM((BLOCKS, 128), jnp.int32),
            pltpu.VMEM((256, 128), F32),
            pltpu.VMEM((128, 256), BF16),
            pltpu.VMEM((CHUNKS // 2, PEERS, 8, 256), F32),
            pltpu.VMEM((256, 256), F32),
            pltpu.VMEM((256, 256), F32),
            pltpu.VMEM((HOLDERS * 8, 256), F32),
            pltpu.VMEM((PLANES * 8, 256), F32),
            dma((4,)),
            pltpu.SemaphoreType.REGULAR((2,)),
            dma, dma((CHUNKS,)),
            dma, dma((CHUNKS, 4)),
            dma, dma,
            dma, dma, dma, dma, dma, dma,
        ],
        compiler_params=pltpu.CompilerParams(
            collective_id=0, has_side_effects=True, vmem_limit_bytes=52 << 20
        ),
        cost_estimate=pl.CostEstimate(flops=2 * 10**9, bytes_accessed=4 << 20, transcendentals=0),
    )(design.reshape(CHUNKS, 256, width), small)


def solution(mesh):
    return jax.shard_map(
        shards,
        mesh=mesh,
        in_specs=(P(("grp", "dev"), None), P(("grp", "dev")), P("grp", None)),
        out_specs=(P(("grp", "dev"), None), P()),
        check_vma=False,
    )
```

```python
import functools
import math

import jax
import jax.numpy as jnp
from jax import lax
from jax.experimental import pallas as pl
from jax.experimental.pallas import tpu as pltpu
from jax.sharding import PartitionSpec as P

MESH = pl.DeviceIdType.MESH
F32 = jnp.float32
BF16 = jnp.bfloat16

GROUPS = 4
PLANES = 8
PEERS = 8
CHUNKS = 8
UNITS = 2 * CHUNKS
IN_RANGE = 32
SLOTS = 4
BLOCKS = 64
HOLDERS = 32
FAR_FIRST = tuple(k ^ 20 for k in range(HOLDERS) if k != 20)
LAG = 4


def butterfly(parts):
    span = 1
    while span < len(parts):
        out = list(parts)
        for a in range(len(parts)):
            if a & span == 0:
                out[a] = parts[a] + parts[a + span]
                out[a + span] = parts[a] - parts[a + span]
        parts = out
        span *= 2
    return parts


def split2(value):
    high = value.astype(BF16)
    return high, (value - high.astype(F32)).astype(BF16)


def dot(a, b):
    return jnp.dot(a, b, preferred_element_type=F32)


def dot_first(a, b):
    return lax.dot_general(a, b, (((0,), (0,)), ((), ())), preferred_element_type=F32)


def kernel(
    scale, gram_scale,
    design, samples_in, bits_in, sketch, gram,
    small,    held, signs, table, arrived, partial, ring, code, owner, code_wide, pick,
    staged, slots, local, part_in, z_in,
    load_sem, ready, y_send, y_recv, z_send, z_recv, d_send, d_recv,
    a_send, a_recv, b_send, b_recv, c_send, c_recv,
):
    g = lax.axis_index("grp")
    dev = lax.axis_index("dev")
    z = dev >> 3
    p = dev & 7
    holder = g * PEERS + p

    def holder_id(k):
        return (g ^ (k >> 3), dev ^ (k & 7))

    loads = [
        pltpu.make_async_copy(
            design.at[:, pl.ds(i * 64, 64), pl.ds(half * 128, 128)],
            held.at[:, half, pl.ds(i * 64, 64)],
            load_sem.at[2 * i + half],
        )
        for i in range(4)
        for half in range(2)
    ]
    small_loads = [
        pltpu.make_async_copy(bits_in, small.at[pl.ds(BLOCKS, 16)], load_sem.at[8]),
        pltpu.make_async_copy(samples_in, small.at[pl.ds(0, BLOCKS)], load_sem.at[9]),
    ]
    for load in small_loads + loads:
        load.start()

    z_next = [(g, (dev + k * PEERS) & 63) for k in (1, PLANES - 1)]
    x_next = [((g + k) & (GROUPS - 1), dev) for k in (1, GROUPS - 1)]
    barrier = pltpu.get_barrier_semaphore()
    for peer in [(g, dev ^ k) for k in (4, 5, 2, 3, 6, 7, 1)] + z_next + x_next:
        pl.semaphore_signal(barrier, inc=1, device_id=peer, device_id_type=MESH)

    for load in small_loads:
        load.wait()

    lane = lax.broadcasted_iota(jnp.int32, (128, 128), 1)
    row = lax.broadcasted_iota(jnp.int32, (128, 128), 0)
    ones = jnp.ones((128, 128), BF16)
    for i in range(16):
        sign = (2 * small[pl.ds(BLOCKS + i, 1), :] - 1).astype(F32)
        diagonal = jnp.where(lane == row, jnp.broadcast_to(sign, (128, 128)), 0.0)
        signs[pl.ds(i * 128, 128), :] = dot(diagonal.astype(BF16), ones)

    target = small[pl.ds(0, BLOCKS), :]
    owner[...] = (target >> 5) & 63
    along_z = (target >> 14) & z
    flip = (along_z ^ (along_z >> 1) ^ (along_z >> 2)) & 1
    code[...] = ((((target >> 11) & 7) << 5) | (target & 31) | (flip << 8) | 512).astype(F32)

    for i in range(8):
        part = pl.ds(i * IN_RANGE, IN_RANGE)
        for half in range(2):
            if i % 2 == 0:
                loads[i + half].wait()
            parts = [held[k, half, part, :] * signs[pl.ds(k * 256 + i * IN_RANGE, IN_RANGE), :] for k in range(8)]
            for k, value in enumerate(butterfly(parts)):
                held[k, half, part, :] = value

    def y_copy(u, k):
        peer = p ^ k
        return pltpu.make_async_remote_copy(
            held.at[u >> 1, u & 1, pl.ds(pl.multiple_of(peer * IN_RANGE, IN_RANGE), IN_RANGE)],
            arrived.at[u, pl.ds(pl.multiple_of(p * IN_RANGE, IN_RANGE), IN_RANGE)],
            y_send, y_recv.at[u],
            device_id=(g, dev ^ k), device_id_type=MESH,
        )

    def wait_bytes(ref, sem):
        pltpu.make_async_copy(ref, ref, sem).wait()

    def low_bits(u, carry):
        parts = [held[u >> 1, u & 1, pl.ds(k * IN_RANGE, IN_RANGE), :] for k in range(8)]
        for k, value in enumerate(butterfly(parts)):
            held[u >> 1, u & 1, pl.ds(k * IN_RANGE, IN_RANGE), :] = value

        @pl.when(u == 0)
        def _():
            pl.semaphore_wait(barrier, PEERS - 1 + 2 + 2)

        for k in (4, 5, 2, 3, 6, 7, 1):
            y_copy(u, k).start()
        mine = pl.multiple_of(p * IN_RANGE, IN_RANGE)
        arrived[u, pl.ds(mine, IN_RANGE), :] = held[u >> 1, u & 1, pl.ds(mine, IN_RANGE), :]
        return carry

    lax.fori_loop(0, UNITS, low_bits, 0)

    for stage in range(2):
        for peer in x_next:
            pl.semaphore_signal(ready.at[stage], inc=1, device_id=peer, device_id_type=MESH)
        if stage == 0:
            pl.semaphore_wait(ready.at[0], 2)

    before = (row < lane).astype(BF16)

    def build(j, carry):
        here = owner[...] == 8 * j + p
        rank = dot(here.astype(F32).astype(BF16), before)
        for i in range(SLOTS):
            chosen = jnp.where(here & (rank == float(i)), code[...], 0.0)
            column = jnp.sum(chosen, axis=1, keepdims=True)
            code_wide[pl.ds(i, BLOCKS, stride=SLOTS), :] = jnp.broadcast_to(column, (BLOCKS, 128))
        wide = code_wide[...].astype(jnp.int32)
        at = lax.broadcasted_iota(jnp.int32, (256, 128), 1) + 256
        for half in range(2):
            v = wide & (at + 128 * half)
            v = v ^ (v >> 8)
            v = v ^ (v >> 4)
            v = v ^ (v >> 2)
            v = v ^ (v >> 1)
            value = jnp.where(wide >= 512, 1 - 2 * (v & 1), 0).astype(F32)
            table[j, :, pl.ds(half * 128, 128)] = value.astype(BF16)
        return carry

    lax.fori_loop(0, CHUNKS, build, 0)

    own = jnp.broadcast_to((small[pl.ds(dev, 1), :] >> 5) & 63, (128, 128)).astype(F32)
    same = jnp.where((own == own.T) & (row < lane), 1.0, 0.0)
    rank = jnp.broadcast_to(jnp.sum(same, axis=0, keepdims=True), (128, 128))
    own = own.astype(jnp.int32)
    place = ((own & 7) * 32 + (own >> 3) * 4).astype(F32) + rank
    place = place.T
    for half in range(2):
        at = (lane + 128 * half).astype(F32)
        pick[:, pl.ds(half * 128, 128)] = jnp.where(place == at, 1.0, 0.0).astype(BF16)

    local[...] = jnp.zeros_like(local)

    def block(index):
        return pl.ds(pl.multiple_of(index * 32, 32), 32)

    def hop(u, way, step, source):
        return pltpu.make_async_remote_copy(
            source, ring.at[u, step, way], z_send, z_recv.at[u, step],
            device_id=z_next[way], device_id_type=MESH,
        )

    def reach(u, way):
        return 3 + ((u + way + 1) & 1)

    def dest(u, way, step):
        far = reach(u, way) - step
        return (z + far) & 7 if way == 0 else (z - far) & 7

    def produce(u):
        wait_bytes(arrived.at[u, pl.ds(0, (PEERS - 1) * IN_RANGE)], y_recv.at[u])
        high, low = split2(arrived[u])
        partial[u] = dot(table[u >> 1], high) + dot(table[u >> 1], low)
        for way in range(2):
            hop(u, way, 0, partial.at[u, block(dest(u, way, 0))]).start()

    def deliver(m, k):
        peer = p ^ k
        return pltpu.make_async_remote_copy(
            staged.at[m, peer], slots.at[pl.ds(pl.multiple_of(p * 32 + m * 8, 8), 8)],
            d_send, d_recv,
            device_id=(g, dev ^ k), device_id_type=MESH,
        )

    def send_pair(m):
        for k in (4, 5, 2, 3, 6, 7, 1):
            deliver(m, k).start()
        slots[pl.ds(pl.multiple_of(p * 32 + m * 8, 8), 8), :] = staged[m, p]

    def forward(u, step):
        if step < 4:
            wait_bytes(ring.at[u, step - 1], z_recv.at[u, step - 1])
        else:
            wait_bytes(ring.at[u, 3, 0], z_recv.at[u, 3])
        for way in range(2):
            def send(way=way):
                ring[u, step - 1, way] += partial[u, block(dest(u, way, step)), :]
                hop(u, way, step, ring.at[u, step - 1, way]).start()

            if step <= 2:
                send()
            elif step == 3:
                pl.when(reach(u, way) == 4)(send)

    def finish(j):
        m = j >> 1
        halves = []
        for half in range(2):
            u = 2 * j + half
            done = partial[u, block(z), :]
            for way in range(2):
                done = done + ring[u, reach(u, way) - 1, way]
            halves.append(done)
        done = jnp.concatenate(halves, axis=1)
        high, low = split2(done)
        local[...] += dot_first(high, high) + dot_first(high, low) + dot_first(low, high)
        for odd in range(2):

            @pl.when((j & 1) == odd)
            def _(odd=odd):
                for k in range(PEERS):
                    staged[m, k, pl.ds(odd * SLOTS, SLOTS), :] = done[k * SLOTS : (k + 1) * SLOTS, :]

        @pl.when(((j & 1) == 1) & (j < CHUNKS - 1))
        def _():
            send_pair(m)

    def turn(t, carry):
        for step in range(1, 5):
            u = t - LAG * step

            @pl.when((u >= 0) & (u < UNITS))
            def _(u=u, step=step):
                forward(u, step)
                if step == 4:
                    pl.when((u & 1) == 1)(lambda: finish(u >> 1))

        @pl.when(t < UNITS)
        def _():
            produce(t)

        return carry

    lax.fori_loop(0, UNITS + 4 * LAG, turn, 0)

    def rows(index):
        return pl.ds(pl.multiple_of(index * 8, 8), 8)

    def copy_a(k):
        return pltpu.make_async_remote_copy(
            local.at[rows(holder ^ k)], part_in.at[rows(holder)], a_send, a_recv,
            device_id=holder_id(k), device_id_type=MESH,
        )

    def copy_b(k):
        return pltpu.make_async_remote_copy(
            z_in.at[rows(z)], z_in.at[rows(z)], b_send, b_recv,
            device_id=(g, dev ^ (k << 3)), device_id_type=MESH,
        )

    def copy_c(k):
        return pltpu.make_async_remote_copy(
            gram.at[rows(holder)], gram.at[rows(holder)], c_send, c_recv,
            device_id=holder_id(k), device_id_type=MESH,
        )

    def wait_all(ref, count, sem):
        wait_bytes(ref.at[pl.ds(0, count * 8)], sem)

    pl.semaphore_wait(ready.at[1], 2)
    for k in FAR_FIRST:
        copy_a(k).start()
    part_in[rows(holder), :] = local[rows(holder), :]
    wait_bytes(held.at[pl.ds(0, PEERS - 1)], y_send)
    wait_bytes(partial.at[pl.ds(0, 2 * (PLANES - 1))], z_send)

    wait_all(part_in, HOLDERS - 1, a_recv)
    z_in[rows(z), :] = jnp.sum(part_in[...].reshape(HOLDERS, 8, 256), axis=0)
    for k in (4, 3, 5, 2, 6, 1, 7):
        copy_b(k).start()
    send_pair(CHUNKS // 2 - 1)
    wait_all(part_in, HOLDERS - 1, a_send)
    wait_all(z_in, PLANES - 1, b_recv)
    gram[rows(holder), :] = jnp.sum(z_in[...].reshape(PLANES, 8, 256), axis=0) * gram_scale
    for k in FAR_FIRST:
        copy_c(k).start()
    wait_bytes(slots.at[pl.ds(0, (PEERS - 1) * 32)], d_recv)
    wait_bytes(slots.at[pl.ds(0, (PEERS - 1) * 32)], d_send)
    value = slots[...]
    first, rest = split2(value)
    second, third = split2(value - first.astype(F32))
    sketch[...] = (dot(pick[...], first) + dot(pick[...], second) + dot(pick[...], third)) * scale

    wait_all(z_in, PLANES - 1, b_send)
    wait_all(gram, HOLDERS - 1, c_recv)
    wait_all(gram, HOLDERS - 1, c_send)


def shards(design, sign_bits, sample_rows):
    rows, width = design.shape
    slab = rows * lax.axis_size("dev")
    total = lax.axis_size("grp") * sample_rows.shape[1]
    vmem = pl.BlockSpec(memory_space=pltpu.VMEM)
    hbm = pl.BlockSpec(memory_space=pltpu.HBM)
    operands = [
        pltpu.with_memory_space_constraint(x, pltpu.HBM)
        for x in (
            design.reshape(CHUNKS, 256, width),
            sample_rows.reshape(BLOCKS, 128),
            sign_bits.reshape(16, 128),
        )
    ]
    dma = pltpu.SemaphoreType.DMA
    return pl.pallas_call(
        functools.partial(kernel, 1.0 / math.sqrt(slab), 1.0 / (slab * total)),
        out_shape=(
            jax.ShapeDtypeStruct((128, width), F32),
            jax.ShapeDtypeStruct((width, width), F32),
        ),
        in_specs=[hbm, hbm, hbm],
        out_specs=(vmem, vmem),
        scratch_shapes=[
            pltpu.VMEM((BLOCKS + 16, 128), jnp.int32),
            pltpu.VMEM((CHUNKS, 2, 256, 128), F32),
            pltpu.VMEM((2048, 128), F32),
            pltpu.VMEM((CHUNKS, 256, 256), BF16),
            pltpu.VMEM((UNITS, 256, 128), F32),
            pltpu.VMEM((UNITS, 256, 128), F32),
            pltpu.VMEM((UNITS, 4, 2, 32, 128), F32),
            pltpu.VMEM((BLOCKS, 128), F32),
            pltpu.VMEM((BLOCKS, 128), jnp.int32),
            pltpu.VMEM((256, 128), F32),
            pltpu.VMEM((128, 256), BF16),
            pltpu.VMEM((CHUNKS // 2, PEERS, 8, 256), F32),
            pltpu.VMEM((256, 256), F32),
            pltpu.VMEM((256, 256), F32),
            pltpu.VMEM((HOLDERS * 8, 256), F32),
            pltpu.VMEM((PLANES * 8, 256), F32),
            dma((10,)),
            pltpu.SemaphoreType.REGULAR((2,)),
            dma, dma((UNITS,)),
            dma, dma((UNITS, 4)),
            dma, dma,
            dma, dma, dma, dma, dma, dma,
        ],
        compiler_params=pltpu.CompilerParams(
            collective_id=0, has_side_effects=True, vmem_limit_bytes=52 << 20
        ),
        cost_estimate=pl.CostEstimate(flops=2 * 10**9, bytes_accessed=4 << 20, transcendentals=0),
    )(*operands)


def solution(mesh):
    return jax.shard_map(
        shards,
        mesh=mesh,
        in_specs=(P(("grp", "dev"), None), P(("grp", "dev")), P("grp", None)),
        out_specs=(P(("grp", "dev"), None), P()),
        check_vma=False,
    )
```

```python
import functools
import math

import jax
import jax.numpy as jnp
from jax import lax
from jax.experimental import pallas as pl
from jax.experimental.pallas import tpu as pltpu
from jax.sharding import PartitionSpec as P

MESH = pl.DeviceIdType.MESH
F32 = jnp.float32
BF16 = jnp.bfloat16

GROUPS = 4
PLANES = 8
PEERS = 8
CHUNKS = 8
UNITS = 2 * CHUNKS
IN_RANGE = 32
SLOTS = 4
BLOCKS = 64
HOLDERS = 32
FAR_FIRST = tuple(k ^ 20 for k in range(HOLDERS) if k != 20)
LAG = 4


def hops(k):
    along = (0, 1, 2, 1)
    return 10 * (along[k >> 3] + along[(k >> 1) & 3]) + (k & 1)


def butterfly(parts):
    span = 1
    while span < len(parts):
        out = list(parts)
        for a in range(len(parts)):
            if a & span == 0:
                out[a] = parts[a] + parts[a + span]
                out[a + span] = parts[a] - parts[a + span]
        parts = out
        span *= 2
    return parts


def split2(value):
    high = value.astype(BF16)
    return high, (value - high.astype(F32)).astype(BF16)


def dot(a, b):
    return jnp.dot(a, b, preferred_element_type=F32)


def dot_first(a, b):
    return lax.dot_general(a, b, (((0,), (0,)), ((), ())), preferred_element_type=F32)


def kernel(
    scale, gram_scale,
    design, samples_in, bits_in, sketch, gram,
    small,    held, signs, table, arrived, partial, ring, code, owner, code_wide, pick,
    staged, slots, local, part_in, z_in,
    load_sem, ready, y_send, y_recv, z_send, z_recv, d_send, d_recv,
    a_send, a_recv, b_send, b_recv, c_send, c_recv,
):
    g = lax.axis_index("grp")
    dev = lax.axis_index("dev")
    z = dev >> 3
    p = dev & 7
    holder = g * PEERS + p

    def holder_id(k):
        return (g ^ (k >> 3), dev ^ (k & 7))

    loads = [
        pltpu.make_async_copy(
            design.at[:, pl.ds(i * 64, 64), pl.ds(half * 128, 128)],
            held.at[:, half, pl.ds(i * 64, 64)],
            load_sem.at[2 * i + half],
        )
        for i in range(4)
        for half in range(2)
    ]
    small_loads = [
        pltpu.make_async_copy(bits_in, small.at[pl.ds(BLOCKS, 16)], load_sem.at[8]),
        pltpu.make_async_copy(samples_in, small.at[pl.ds(0, BLOCKS)], load_sem.at[9]),
    ]
    for load in small_loads + loads:
        load.start()

    z_next = [(g, (dev + k * PEERS) & 63) for k in (1, PLANES - 1)]
    x_next = [((g + k) & (GROUPS - 1), dev) for k in (1, GROUPS - 1)]
    barrier = pltpu.get_barrier_semaphore()
    for peer in [(g, dev ^ k) for k in (4, 5, 2, 3, 6, 7, 1)] + z_next + x_next:
        pl.semaphore_signal(barrier, inc=1, device_id=peer, device_id_type=MESH)

    for load in small_loads:
        load.wait()

    lane = lax.broadcasted_iota(jnp.int32, (128, 128), 1)
    row = lax.broadcasted_iota(jnp.int32, (128, 128), 0)
    ones = jnp.ones((128, 128), BF16)
    for i in range(16):
        sign = (2 * small[pl.ds(BLOCKS + i, 1), :] - 1).astype(F32)
        diagonal = jnp.where(lane == row, jnp.broadcast_to(sign, (128, 128)), 0.0)
        signs[pl.ds(i * 128, 128), :] = dot(diagonal.astype(BF16), ones)

    target = small[pl.ds(0, BLOCKS), :]
    owner[...] = (target >> 5) & 63
    along_z = (target >> 14) & z
    flip = (along_z ^ (along_z >> 1) ^ (along_z >> 2)) & 1
    code[...] = ((((target >> 11) & 7) << 5) | (target & 31) | (flip << 8) | 512).astype(F32)

    for i in range(8):
        part = pl.ds(i * IN_RANGE, IN_RANGE)
        for half in range(2):
            if i % 2 == 0:
                loads[i + half].wait()
            parts = [held[k, half, part, :] * signs[pl.ds(k * 256 + i * IN_RANGE, IN_RANGE), :] for k in range(8)]
            for k, value in enumerate(butterfly(parts)):
                held[k, half, part, :] = value

    def y_copy(u, k):
        peer = p ^ k
        return pltpu.make_async_remote_copy(
            held.at[u >> 1, u & 1, pl.ds(pl.multiple_of(peer * IN_RANGE, IN_RANGE), IN_RANGE)],
            arrived.at[u, pl.ds(pl.multiple_of(p * IN_RANGE, IN_RANGE), IN_RANGE)],
            y_send, y_recv.at[u],
            device_id=(g, dev ^ k), device_id_type=MESH,
        )

    def wait_bytes(ref, sem):
        pltpu.make_async_copy(ref, ref, sem).wait()

    def low_bits(u, carry):
        parts = [held[u >> 1, u & 1, pl.ds(k * IN_RANGE, IN_RANGE), :] for k in range(8)]
        for k, value in enumerate(butterfly(parts)):
            held[u >> 1, u & 1, pl.ds(k * IN_RANGE, IN_RANGE), :] = value

        @pl.when(u == 0)
        def _():
            pl.semaphore_wait(barrier, PEERS - 1 + 2 + 2)

        for k in (4, 5, 2, 3, 6, 7, 1):
            y_copy(u, k).start()
        mine = pl.multiple_of(p * IN_RANGE, IN_RANGE)
        arrived[u, pl.ds(mine, IN_RANGE), :] = held[u >> 1, u & 1, pl.ds(mine, IN_RANGE), :]
        return carry

    lax.fori_loop(0, UNITS, low_bits, 0)

    for stage in range(2):
        for peer in x_next:
            pl.semaphore_signal(ready.at[stage], inc=1, device_id=peer, device_id_type=MESH)
        if stage == 0:
            pl.semaphore_wait(ready.at[0], 2)

    before = (row < lane).astype(BF16)

    def build(j, carry):
        here = owner[...] == 8 * j + p
        rank = dot(here.astype(F32).astype(BF16), before)
        for i in range(SLOTS):
            chosen = jnp.where(here & (rank == float(i)), code[...], 0.0)
            column = jnp.sum(chosen, axis=1, keepdims=True)
            code_wide[pl.ds(i, BLOCKS, stride=SLOTS), :] = jnp.broadcast_to(column, (BLOCKS, 128))
        wide = code_wide[...].astype(jnp.int32)
        at = lax.broadcasted_iota(jnp.int32, (256, 128), 1) + 256
        for half in range(2):
            v = wide & (at + 128 * half)
            v = v ^ (v >> 8)
            v = v ^ (v >> 4)
            v = v ^ (v >> 2)
            v = v ^ (v >> 1)
            value = jnp.where(wide >= 512, 1 - 2 * (v & 1), 0).astype(F32)
            table[j, :, pl.ds(half * 128, 128)] = value.astype(BF16)
        return carry

    lax.fori_loop(0, CHUNKS, build, 0)

    own = jnp.broadcast_to((small[pl.ds(dev, 1), :] >> 5) & 63, (128, 128)).astype(F32)
    same = jnp.where((own == own.T) & (row < lane), 1.0, 0.0)
    rank = jnp.broadcast_to(jnp.sum(same, axis=0, keepdims=True), (128, 128))
    own = own.astype(jnp.int32)
    place = ((own & 7) * 32 + (own >> 3) * 4).astype(F32) + rank
    place = place.T
    for half in range(2):
        at = (lane + 128 * half).astype(F32)
        pick[:, pl.ds(half * 128, 128)] = jnp.where(place == at, 1.0, 0.0).astype(BF16)

    local[...] = jnp.zeros_like(local)

    def block(index):
        return pl.ds(pl.multiple_of(index * 32, 32), 32)

    def hop(u, way, step, source):
        return pltpu.make_async_remote_copy(
            source, ring.at[u, step, way], z_send, z_recv.at[u, step],
            device_id=z_next[way], device_id_type=MESH,
        )

    def reach(u, way):
        return 3 + ((u + way + 1) & 1)

    def dest(u, way, step):
        far = reach(u, way) - step
        return (z + far) & 7 if way == 0 else (z - far) & 7

    def produce(u):
        wait_bytes(arrived.at[u, pl.ds(0, (PEERS - 1) * IN_RANGE)], y_recv.at[u])
        high, low = split2(arrived[u])
        both = dot(table[u >> 1], jnp.concatenate([high, low], axis=1))
        partial[u] = both[:, :128] + both[:, 128:]
        for way in range(2):
            hop(u, way, 0, partial.at[u, block(dest(u, way, 0))]).start()

    def deliver(m, k):
        peer = p ^ k
        return pltpu.make_async_remote_copy(
            staged.at[m, peer], slots.at[pl.ds(pl.multiple_of(p * 32 + m * 8, 8), 8)],
            d_send, d_recv,
            device_id=(g, dev ^ k), device_id_type=MESH,
        )

    def send_pair(m):
        for k in (4, 5, 2, 3, 6, 7, 1):
            deliver(m, k).start()
        slots[pl.ds(pl.multiple_of(p * 32 + m * 8, 8), 8), :] = staged[m, p]

    def forward(u, step):
        if step < 4:
            wait_bytes(ring.at[u, step - 1], z_recv.at[u, step - 1])
        else:
            wait_bytes(ring.at[u, 3, 0], z_recv.at[u, 3])
        for way in range(2):
            def send(way=way):
                ring[u, step - 1, way] += partial[u, block(dest(u, way, step)), :]
                hop(u, way, step, ring.at[u, step - 1, way]).start()

            if step <= 2:
                send()
            elif step == 3:
                pl.when(reach(u, way) == 4)(send)

    def finish(j):
        m = j >> 1
        halves = []
        for half in range(2):
            u = 2 * j + half
            done = partial[u, block(z), :]
            for way in range(2):
                done = done + ring[u, reach(u, way) - 1, way]
            halves.append(done)
        done = jnp.concatenate(halves, axis=1)
        high, low = split2(done)
        local[...] += dot_first(
            jnp.concatenate([high, high, low], axis=0), jnp.concatenate([high, low, high], axis=0)
        )
        for odd in range(2):

            @pl.when((j & 1) == odd)
            def _(odd=odd):
                for k in range(PEERS):
                    staged[m, k, pl.ds(odd * SLOTS, SLOTS), :] = done[k * SLOTS : (k + 1) * SLOTS, :]

        @pl.when(((j & 1) == 1) & (j < CHUNKS - 1))
        def _():
            send_pair(m)

    def turn(t, carry):
        for step in range(1, 5):
            u = t - LAG * step

            @pl.when((u >= 0) & (u < UNITS))
            def _(u=u, step=step):
                forward(u, step)
                if step == 4:
                    pl.when((u & 1) == 1)(lambda: finish(u >> 1))

        @pl.when(t < UNITS)
        def _():
            produce(t)

        return carry

    lax.fori_loop(0, UNITS + 4 * LAG, turn, 0)

    def rows(index):
        return pl.ds(pl.multiple_of(index * 8, 8), 8)

    def copy_a(k):
        return pltpu.make_async_remote_copy(
            local.at[rows(holder ^ k)], part_in.at[rows(holder)], a_send, a_recv,
            device_id=holder_id(k), device_id_type=MESH,
        )

    def copy_b(k):
        return pltpu.make_async_remote_copy(
            z_in.at[rows(z)], z_in.at[rows(z)], b_send, b_recv,
            device_id=(g, dev ^ (k << 3)), device_id_type=MESH,
        )

    def copy_c(k):
        return pltpu.make_async_remote_copy(
            gram.at[rows(holder)], gram.at[rows(holder)], c_send, c_recv,
            device_id=holder_id(k), device_id_type=MESH,
        )

    def wait_all(ref, count, sem):
        wait_bytes(ref.at[pl.ds(0, count * 8)], sem)

    pl.semaphore_wait(ready.at[1], 2)
    for k in sorted(FAR_FIRST, key=hops, reverse=True):
        copy_a(k).start()
    part_in[rows(holder), :] = local[rows(holder), :]
    wait_bytes(held.at[pl.ds(0, PEERS - 1)], y_send)
    wait_bytes(partial.at[pl.ds(0, 2 * (PLANES - 1))], z_send)

    wait_all(part_in, HOLDERS - 1, a_recv)
    z_in[rows(z), :] = jnp.sum(part_in[...].reshape(HOLDERS, 8, 256), axis=0)
    for k in (4, 3, 5, 2, 6, 1, 7):
        copy_b(k).start()
    send_pair(CHUNKS // 2 - 1)
    wait_all(part_in, HOLDERS - 1, a_send)
    wait_all(z_in, PLANES - 1, b_recv)
    gram[rows(holder), :] = jnp.sum(z_in[...].reshape(PLANES, 8, 256), axis=0) * gram_scale
    for k in sorted(FAR_FIRST, key=hops, reverse=True):
        copy_c(k).start()
    wait_bytes(slots.at[pl.ds(0, (PEERS - 1) * 32)], d_recv)
    wait_bytes(slots.at[pl.ds(0, (PEERS - 1) * 32)], d_send)
    value = slots[...]
    first, rest = split2(value)
    second, third = split2(value - first.astype(F32))
    sketch[...] = (dot(pick[...], first) + dot(pick[...], second) + dot(pick[...], third)) * scale

    wait_all(z_in, PLANES - 1, b_send)
    wait_all(gram, HOLDERS - 1, c_recv)
    wait_all(gram, HOLDERS - 1, c_send)


def shards(design, sign_bits, sample_rows):
    rows, width = design.shape
    slab = rows * lax.axis_size("dev")
    total = lax.axis_size("grp") * sample_rows.shape[1]
    vmem = pl.BlockSpec(memory_space=pltpu.VMEM)
    hbm = pl.BlockSpec(memory_space=pltpu.HBM)
    operands = [
        pltpu.with_memory_space_constraint(x, pltpu.HBM)
        for x in (
            design.reshape(CHUNKS, 256, width),
            sample_rows.reshape(BLOCKS, 128),
            sign_bits.reshape(16, 128),
        )
    ]
    dma = pltpu.SemaphoreType.DMA
    return pl.pallas_call(
        functools.partial(kernel, 1.0 / math.sqrt(slab), 1.0 / (slab * total)),
        out_shape=(
            jax.ShapeDtypeStruct((128, width), F32),
            jax.ShapeDtypeStruct((width, width), F32),
        ),
        in_specs=[hbm, hbm, hbm],
        out_specs=(vmem, vmem),
        scratch_shapes=[
            pltpu.VMEM((BLOCKS + 16, 128), jnp.int32),
            pltpu.VMEM((CHUNKS, 2, 256, 128), F32),
            pltpu.VMEM((2048, 128), F32),
            pltpu.VMEM((CHUNKS, 256, 256), BF16),
            pltpu.VMEM((UNITS, 256, 128), F32),
            pltpu.VMEM((UNITS, 256, 128), F32),
            pltpu.VMEM((UNITS, 4, 2, 32, 128), F32),
            pltpu.VMEM((BLOCKS, 128), F32),
            pltpu.VMEM((BLOCKS, 128), jnp.int32),
            pltpu.VMEM((256, 128), F32),
            pltpu.VMEM((128, 256), BF16),
            pltpu.VMEM((CHUNKS // 2, PEERS, 8, 256), F32),
            pltpu.VMEM((256, 256), F32),
            pltpu.VMEM((256, 256), F32),
            pltpu.VMEM((HOLDERS * 8, 256), F32),
            pltpu.VMEM((PLANES * 8, 256), F32),
            dma((10,)),
            pltpu.SemaphoreType.REGULAR((2,)),
            dma, dma((UNITS,)),
            dma, dma((UNITS, 4)),
            dma, dma,
            dma, dma, dma, dma, dma, dma,
        ],
        compiler_params=pltpu.CompilerParams(
            collective_id=0, has_side_effects=True, vmem_limit_bytes=52 << 20
        ),
        cost_estimate=pl.CostEstimate(flops=2 * 10**9, bytes_accessed=4 << 20, transcendentals=0),
    )(*operands)


def solution(mesh):
    return jax.shard_map(
        shards,
        mesh=mesh,
        in_specs=(P(("grp", "dev"), None), P(("grp", "dev")), P("grp", None)),
        out_specs=(P(("grp", "dev"), None), P()),
        check_vma=False,
    )
```

```python
import functools
import math

import jax
import jax.numpy as jnp
from jax import lax
from jax.experimental import pallas as pl
from jax.experimental.pallas import tpu as pltpu
from jax.sharding import PartitionSpec as P

MESH = pl.DeviceIdType.MESH
F32 = jnp.float32
BF16 = jnp.bfloat16

GROUPS = 4
PLANES = 8
PEERS = 8
CHUNKS = 8
UNITS = 2 * CHUNKS
IN_RANGE = 32
SLOTS = 4
BLOCKS = 64
HOLDERS = 32
FAR_FIRST = tuple(k ^ 20 for k in range(HOLDERS) if k != 20)
LAG = 4


def hops(k):
    along = (0, 1, 2, 1)
    return 10 * (along[k >> 3] + along[(k >> 1) & 3]) + (k & 1)


def butterfly(parts):
    span = 1
    while span < len(parts):
        out = list(parts)
        for a in range(len(parts)):
            if a & span == 0:
                out[a] = parts[a] + parts[a + span]
                out[a + span] = parts[a] - parts[a + span]
        parts = out
        span *= 2
    return parts


def split2(value):
    high = value.astype(BF16)
    return high, (value - high.astype(F32)).astype(BF16)


def dot(a, b):
    return jnp.dot(a, b, preferred_element_type=F32)


def dot_first(a, b):
    return lax.dot_general(a, b, (((0,), (0,)), ((), ())), preferred_element_type=F32)


def kernel(
    scale, gram_scale,
    design, samples_in, bits_in, sketch, gram,
    small,    held, signs, table, arrived, partial, ring, code, owner, code_wide, pick,
    staged, slots, local, part_in, z_in,
    load_sem, ready, y_send, y_recv, z_send, z_recv, d_send, d_recv,
    a_send, a_recv, b_send, b_recv, c_send, c_recv,
):
    g = lax.axis_index("grp")
    dev = lax.axis_index("dev")
    z = dev >> 3
    p = dev & 7
    holder = g * PEERS + p

    def holder_id(k):
        return (g ^ (k >> 3), dev ^ (k & 7))

    loads = [
        pltpu.make_async_copy(
            design.at[:, pl.ds(i * 64, 64), pl.ds(half * 128, 128)],
            held.at[:, half, pl.ds(i * 64, 64)],
            load_sem.at[2 * i + half],
        )
        for i in range(4)
        for half in range(2)
    ]
    small_loads = [
        pltpu.make_async_copy(bits_in, small.at[pl.ds(BLOCKS, 16)], load_sem.at[8]),
        pltpu.make_async_copy(samples_in, small.at[pl.ds(0, BLOCKS)], load_sem.at[9]),
    ]

    z_next = [(g, (dev + k * PEERS) & 63) for k in (1, PLANES - 1)]
    x_next = [((g + k) & (GROUPS - 1), dev) for k in (1, GROUPS - 1)]
    barrier = pltpu.get_barrier_semaphore()
    for peer in [(g, dev ^ k) for k in (4, 5, 2, 3, 6, 7, 1)] + z_next + x_next:
        pl.semaphore_signal(barrier, inc=1, device_id=peer, device_id_type=MESH)
    for load in small_loads + loads:
        load.start()

    for load in small_loads:
        load.wait()

    lane = lax.broadcasted_iota(jnp.int32, (128, 128), 1)
    row = lax.broadcasted_iota(jnp.int32, (128, 128), 0)
    ones = jnp.ones((128, 128), BF16)
    for i in range(16):
        sign = (2 * small[pl.ds(BLOCKS + i, 1), :] - 1).astype(F32)
        diagonal = jnp.where(lane == row, jnp.broadcast_to(sign, (128, 128)), 0.0)
        signs[pl.ds(i * 128, 128), :] = dot(diagonal.astype(BF16), ones)

    target = small[pl.ds(0, BLOCKS), :]
    owner[...] = (target >> 5) & 63
    along_z = (target >> 14) & z
    flip = (along_z ^ (along_z >> 1) ^ (along_z >> 2)) & 1
    code[...] = ((((target >> 11) & 7) << 5) | (target & 31) | (flip << 8) | 512).astype(F32)

    for i in range(8):
        part = pl.ds(i * IN_RANGE, IN_RANGE)
        for half in range(2):
            if i % 2 == 0:
                loads[i + half].wait()
            parts = [held[k, half, part, :] * signs[pl.ds(k * 256 + i * IN_RANGE, IN_RANGE), :] for k in range(8)]
            for k, value in enumerate(butterfly(parts)):
                held[k, half, part, :] = value

    def y_copy(u, k):
        peer = p ^ k
        return pltpu.make_async_remote_copy(
            held.at[u >> 1, u & 1, pl.ds(pl.multiple_of(peer * IN_RANGE, IN_RANGE), IN_RANGE)],
            arrived.at[u, pl.ds(pl.multiple_of(p * IN_RANGE, IN_RANGE), IN_RANGE)],
            y_send, y_recv.at[u],
            device_id=(g, dev ^ k), device_id_type=MESH,
        )

    def wait_bytes(ref, sem):
        pltpu.make_async_copy(ref, ref, sem).wait()

    def low_bits(u, carry):
        parts = [held[u >> 1, u & 1, pl.ds(k * IN_RANGE, IN_RANGE), :] for k in range(8)]
        for k, value in enumerate(butterfly(parts)):
            held[u >> 1, u & 1, pl.ds(k * IN_RANGE, IN_RANGE), :] = value

        @pl.when(u == 0)
        def _():
            pl.semaphore_wait(barrier, PEERS - 1 + 2 + 2)

        for k in (4, 5, 2, 3, 6, 7, 1):
            y_copy(u, k).start()
        mine = pl.multiple_of(p * IN_RANGE, IN_RANGE)
        arrived[u, pl.ds(mine, IN_RANGE), :] = held[u >> 1, u & 1, pl.ds(mine, IN_RANGE), :]
        return carry

    lax.fori_loop(0, UNITS, low_bits, 0)

    for stage in range(2):
        for peer in x_next:
            pl.semaphore_signal(ready.at[stage], inc=1, device_id=peer, device_id_type=MESH)
        if stage == 0:
            pl.semaphore_wait(ready.at[0], 2)

    before = (row < lane).astype(BF16)

    def build(j, carry):
        here = owner[...] == 8 * j + p
        rank = dot(here.astype(F32).astype(BF16), before)
        for i in range(SLOTS):
            chosen = jnp.where(here & (rank == float(i)), code[...], 0.0)
            column = jnp.sum(chosen, axis=1, keepdims=True)
            code_wide[pl.ds(i, BLOCKS, stride=SLOTS), :] = jnp.broadcast_to(column, (BLOCKS, 128))
        wide = code_wide[...].astype(jnp.int32)
        at = lax.broadcasted_iota(jnp.int32, (256, 128), 1) + 256
        for half in range(2):
            v = wide & (at + 128 * half)
            v = v ^ (v >> 8)
            v = v ^ (v >> 4)
            v = v ^ (v >> 2)
            v = v ^ (v >> 1)
            value = jnp.where(wide >= 512, 1 - 2 * (v & 1), 0).astype(F32)
            table[j, :, pl.ds(half * 128, 128)] = value.astype(BF16)
        return carry

    lax.fori_loop(0, CHUNKS, build, 0)

    own = jnp.broadcast_to((small[pl.ds(dev, 1), :] >> 5) & 63, (128, 128)).astype(F32)
    same = jnp.where((own == own.T) & (row < lane), 1.0, 0.0)
    rank = jnp.broadcast_to(jnp.sum(same, axis=0, keepdims=True), (128, 128))
    own = own.astype(jnp.int32)
    place = ((own & 7) * 32 + (own >> 3) * 4).astype(F32) + rank
    place = place.T
    for half in range(2):
        at = (lane + 128 * half).astype(F32)
        pick[:, pl.ds(half * 128, 128)] = jnp.where(place == at, 1.0, 0.0).astype(BF16)

    local[...] = jnp.zeros_like(local)

    def block(index):
        return pl.ds(pl.multiple_of(index * 32, 32), 32)

    def hop(u, way, step, source):
        return pltpu.make_async_remote_copy(
            source, ring.at[u, step, way], z_send, z_recv.at[u, step],
            device_id=z_next[way], device_id_type=MESH,
        )

    def reach(u, way):
        return 3 + ((u + way + 1) & 1)

    def dest(u, way, step):
        far = reach(u, way) - step
        return (z + far) & 7 if way == 0 else (z - far) & 7

    def produce(u):
        wait_bytes(arrived.at[u, pl.ds(0, (PEERS - 1) * IN_RANGE)], y_recv.at[u])
        high, low = split2(arrived[u])
        both = dot(table[u >> 1], jnp.concatenate([high, low], axis=1))
        partial[u] = both[:, :128] + both[:, 128:]
        for way in range(2):
            hop(u, way, 0, partial.at[u, block(dest(u, way, 0))]).start()

    def deliver(m, k):
        peer = p ^ k
        return pltpu.make_async_remote_copy(
            staged.at[m, peer], slots.at[pl.ds(pl.multiple_of(p * 32 + m * 8, 8), 8)],
            d_send, d_recv,
            device_id=(g, dev ^ k), device_id_type=MESH,
        )

    def send_pair(m):
        for k in (4, 5, 2, 3, 6, 7, 1):
            deliver(m, k).start()
        slots[pl.ds(pl.multiple_of(p * 32 + m * 8, 8), 8), :] = staged[m, p]

    def forward(u, step):
        if step < 4:
            wait_bytes(ring.at[u, step - 1], z_recv.at[u, step - 1])
        else:
            wait_bytes(ring.at[u, 3, 0], z_recv.at[u, 3])
        for way in range(2):
            def send(way=way):
                ring[u, step - 1, way] += partial[u, block(dest(u, way, step)), :]
                hop(u, way, step, ring.at[u, step - 1, way]).start()

            if step <= 2:
                send()
            elif step == 3:
                pl.when(reach(u, way) == 4)(send)

    def finish(j):
        m = j >> 1
        halves = []
        for half in range(2):
            u = 2 * j + half
            done = partial[u, block(z), :]
            for way in range(2):
                done = done + ring[u, reach(u, way) - 1, way]
            halves.append(done)
        done = jnp.concatenate(halves, axis=1)
        high, low = split2(done)
        local[...] += dot_first(
            jnp.concatenate([high, high, low], axis=0), jnp.concatenate([high, low, high], axis=0)
        )
        for odd in range(2):

            @pl.when((j & 1) == odd)
            def _(odd=odd):
                for k in range(PEERS):
                    staged[m, k, pl.ds(odd * SLOTS, SLOTS), :] = done[k * SLOTS : (k + 1) * SLOTS, :]

        @pl.when(((j & 1) == 1) & (j < CHUNKS - 1))
        def _():
            send_pair(m)

    def turn(t, carry):
        for step in range(1, 5):
            u = t - LAG * step

            @pl.when((u >= 0) & (u < UNITS))
            def _(u=u, step=step):
                forward(u, step)
                if step == 4:
                    pl.when((u & 1) == 1)(lambda: finish(u >> 1))

        @pl.when(t < UNITS)
        def _():
            produce(t)

        return carry

    lax.fori_loop(0, UNITS + 4 * LAG, turn, 0)

    def rows(index):
        return pl.ds(pl.multiple_of(index * 8, 8), 8)

    def copy_a(k):
        return pltpu.make_async_remote_copy(
            local.at[rows(holder ^ k)], part_in.at[rows(holder)], a_send, a_recv,
            device_id=holder_id(k), device_id_type=MESH,
        )

    def copy_b(k):
        return pltpu.make_async_remote_copy(
            z_in.at[rows(z)], z_in.at[rows(z)], b_send, b_recv,
            device_id=(g, dev ^ (k << 3)), device_id_type=MESH,
        )

    def copy_c(k):
        return pltpu.make_async_remote_copy(
            gram.at[rows(holder)], gram.at[rows(holder)], c_send, c_recv,
            device_id=holder_id(k), device_id_type=MESH,
        )

    def wait_all(ref, count, sem):
        wait_bytes(ref.at[pl.ds(0, count * 8)], sem)

    pl.semaphore_wait(ready.at[1], 2)
    for k in sorted(FAR_FIRST, key=hops, reverse=True):
        copy_a(k).start()
    part_in[rows(holder), :] = local[rows(holder), :]
    wait_bytes(held.at[pl.ds(0, PEERS - 1)], y_send)
    wait_bytes(partial.at[pl.ds(0, 2 * (PLANES - 1))], z_send)

    wait_all(part_in, HOLDERS - 1, a_recv)
    z_in[rows(z), :] = jnp.sum(part_in[...].reshape(HOLDERS, 8, 256), axis=0)
    for k in (4, 3, 5, 2, 6, 1, 7):
        copy_b(k).start()
    send_pair(CHUNKS // 2 - 1)
    wait_all(part_in, HOLDERS - 1, a_send)
    wait_all(z_in, PLANES - 1, b_recv)
    gram[rows(holder), :] = jnp.sum(z_in[...].reshape(PLANES, 8, 256), axis=0) * gram_scale
    for k in sorted(FAR_FIRST, key=hops, reverse=True):
        copy_c(k).start()
    wait_bytes(slots.at[pl.ds(0, (PEERS - 1) * 32)], d_recv)
    wait_bytes(slots.at[pl.ds(0, (PEERS - 1) * 32)], d_send)
    value = slots[...]
    first, rest = split2(value)
    second, third = split2(value - first.astype(F32))
    sketch[...] = (dot(pick[...], first) + dot(pick[...], second) + dot(pick[...], third)) * scale

    wait_all(z_in, PLANES - 1, b_send)
    wait_all(gram, HOLDERS - 1, c_recv)
    wait_all(gram, HOLDERS - 1, c_send)


def shards(design, sign_bits, sample_rows):
    rows, width = design.shape
    slab = rows * lax.axis_size("dev")
    total = lax.axis_size("grp") * sample_rows.shape[1]
    vmem = pl.BlockSpec(memory_space=pltpu.VMEM)
    hbm = pl.BlockSpec(memory_space=pltpu.HBM)
    operands = [
        pltpu.with_memory_space_constraint(x, pltpu.HBM)
        for x in (
            design.reshape(CHUNKS, 256, width),
            sample_rows.reshape(BLOCKS, 128),
            sign_bits.reshape(16, 128),
        )
    ]
    dma = pltpu.SemaphoreType.DMA
    return pl.pallas_call(
        functools.partial(kernel, 1.0 / math.sqrt(slab), 1.0 / (slab * total)),
        out_shape=(
            jax.ShapeDtypeStruct((128, width), F32),
            jax.ShapeDtypeStruct((width, width), F32),
        ),
        in_specs=[hbm, hbm, hbm],
        out_specs=(vmem, vmem),
        scratch_shapes=[
            pltpu.VMEM((BLOCKS + 16, 128), jnp.int32),
            pltpu.VMEM((CHUNKS, 2, 256, 128), F32),
            pltpu.VMEM((2048, 128), F32),
            pltpu.VMEM((CHUNKS, 256, 256), BF16),
            pltpu.VMEM((UNITS, 256, 128), F32),
            pltpu.VMEM((UNITS, 256, 128), F32),
            pltpu.VMEM((UNITS, 4, 2, 32, 128), F32),
            pltpu.VMEM((BLOCKS, 128), F32),
            pltpu.VMEM((BLOCKS, 128), jnp.int32),
            pltpu.VMEM((256, 128), F32),
            pltpu.VMEM((128, 256), BF16),
            pltpu.VMEM((CHUNKS // 2, PEERS, 8, 256), F32),
            pltpu.VMEM((256, 256), F32),
            pltpu.VMEM((256, 256), F32),
            pltpu.VMEM((HOLDERS * 8, 256), F32),
            pltpu.VMEM((PLANES * 8, 256), F32),
            dma((10,)),
            pltpu.SemaphoreType.REGULAR((2,)),
            dma, dma((UNITS,)),
            dma, dma((UNITS, 4)),
            dma, dma,
            dma, dma, dma, dma, dma, dma,
        ],
        compiler_params=pltpu.CompilerParams(
            collective_id=0, has_side_effects=True, vmem_limit_bytes=52 << 20
        ),
        cost_estimate=pl.CostEstimate(flops=2 * 10**9, bytes_accessed=4 << 20, transcendentals=0),
    )(*operands)


def solution(mesh):
    return jax.shard_map(
        shards,
        mesh=mesh,
        in_specs=(P(("grp", "dev"), None), P(("grp", "dev")), P("grp", None)),
        out_specs=(P(("grp", "dev"), None), P()),
        check_vma=False,
    )
```
